256 devices in a mesh: dom: 64 (over y, z_hi, x), gp: 4 (over z_lo, core).
Axes of the slice: x: 4, y: 4, z: 8 (z_hi: 4, z_lo: 2; z = z_hi * 2 + z_lo), core: 2. Of those that a mesh axis runs over, the one named last changes fastest.
Arguments:
- atoms: bfloat16 [65536, 512], P(('dom', 'gp')), may hold values from -6 to 6
- messages: bfloat16 [524288, 512], P(('dom', 'gp')), may hold values from -6 to 6
- edge_src: int32 [524288], P(('dom', 'gp')), may hold values from 0 to 2047
- edge_dst: int32 [524288], P(('dom', 'gp')), may hold values from 0 to 1023
- trip_in: int32 [524288], P(('dom', 'gp')), may hold values from 0 to 2047
- trip_out: int32 [524288], P(('dom', 'gp')), may hold values from 0 to 2047
- trip_basis: bfloat16 [524288, 64], P(('dom', 'gp')), may hold values from -6 to 6
- edge_count: int32 [256], P(('dom', 'gp')), may hold values from 256 to 2048, as said below
- trip_count: int32 [256], P(('dom', 'gp')), may hold values from 256 to 2048, as said below
- w_a: bfloat16 [512, 512], replicated, may hold values from -0.25 to 0.25
- w_down: bfloat16 [512, 64], replicated, may hold values from -0.25 to 0.25
- w_t: bfloat16 [64, 512], replicated, may hold values from -0.75 to 0.75
- w_b: bfloat16 [512, 512], replicated, may hold values from -0.25 to 0.25
- cotangent: bfloat16 [65536, 512], P(('dom', 'gp')), may hold values from -6 to 6
Outputs:
- grad_atoms: bfloat16 [65536, 512], P(('dom', 'gp'))
- grad_wa: float32 [512, 512], replicated
- grad_wd: float32 [512, 64], replicated
- grad_wt: float32 [64, 512], replicated
- grad_wb: float32 [512, 512], replicated
The draws below stay inside these ranges and needn't reach their ends.
Inputs may be any that keep to these rules, and one draw needn't show every extreme that they name: `edge_src`: row of the device's slab table: ghost rows of the lower slab, then the slab's 1024 atoms, then ghost rows of the upper slab. `trip_in`: slot of the device's own edges. `trip_out`: slot of the device's own edges. `edge_count`: some device has all 2048 slots valid; counts differ widely between devices. `trip_count`: some device has all 2048 slots valid; counts differ widely between devices.
All inputs are finite; a program needn't handle non-finite values.
Results may differ from the reference program's by a relative error of at most 0.011.
Values may be sent and summed in bfloat16 or wider, within the bound.
A program may use at most 128 MiB of HBM per device.

```python
import math
import jax
import jax.numpy as jnp
from jax import lax

DA = 512
DE = 512
DT = 64
ATOM_DEV = 256
EDGE_DEV = 2048
GH = 128
TRIP_DEV = 2048
A_DOM = 1024
A_EXT = 2048
ATOMS = 65536
EDGES = 524288
TRIPS = 524288
N_DOM = 64
N_GP = 4
DEVICES = 256


def ragged_counts(key, slots):
    first, second = jax.random.split(key)
    level = jax.random.randint(first, (DEVICES,), 0, 64)
    counts = slots // 8 + (slots - slots // 8) * level * level // 3969
    fullest = jax.random.randint(second, (), 0, DEVICES)
    return jnp.where(jnp.arange(DEVICES) == fullest, slots, counts).astype(jnp.int32)


def draw_edge_count(key, part):
    key = jax.random.fold_in(key, 11)
    return ragged_counts(key, EDGE_DEV)


def draw_trip_count(key, part):
    key = jax.random.fold_in(key, 12)
    return ragged_counts(key, TRIP_DEV)


def place_ends(drawn, own_key, low, largest):
    extent = drawn.shape
    index_at = [jax.random.randint(jax.random.fold_in(own_key, axis), (), 0, extent[axis]) for axis in range(len(extent))]
    drawn = drawn.at[tuple(index_at)].set(low)
    longest = extent.index(max(extent))
    index_at[longest] = (index_at[longest] + 1) % extent[longest]
    return drawn.at[tuple(index_at)].set(largest)


def block_scale(own_key, dims, pieces, smallest, top_value):
    gain = 1.0
    for position, parts in pieces:
        steps = jax.random.uniform(jax.random.fold_in(jax.random.fold_in(own_key, 6), position), (parts,), jnp.float32, smallest / len(pieces), top_value / len(pieces))
        gain = gain * jnp.repeat(jnp.exp(steps), dims[position] // parts).reshape((-1,) + (1,) * (len(dims) - 1 - position))
    return gain


def noise(stream_key, dims, spread, most, pieces=(), dtype=jnp.bfloat16):
    result = spread * jax.random.normal(stream_key, dims, jnp.float32)
    if pieces:
        result = result * block_scale(stream_key, dims, pieces, -0.22, 0.18)
    return jnp.clip(result, -most, most).astype(dtype)


def setup_inputs(seed: int = 0) -> dict:
    splits = jax.random.split(jax.random.key(seed), 15)
    return {
        "atoms": noise(splits[0], (ATOMS, DA), 1.0, 6.0, ((0, 256),)),
        "messages": noise(splits[1], (EDGES, DE), 1.0, 6.0, ((0, 256),)),
        "edge_src": place_ends(jax.random.randint(splits[2], (EDGES,), 0, A_EXT), jax.random.fold_in(splits[2], 1), 0, A_EXT - 1).astype(jnp.int32),
        "edge_dst": place_ends(jax.random.randint(splits[3], (EDGES,), 0, A_DOM), jax.random.fold_in(splits[3], 1), 0, A_DOM - 1).astype(jnp.int32),
        "trip_in": place_ends(jax.random.randint(splits[4], (TRIPS,), 0, EDGE_DEV), jax.random.fold_in(splits[4], 1), 0, EDGE_DEV - 1).astype(jnp.int32),
        "trip_out": place_ends(jax.random.randint(splits[5], (TRIPS,), 0, EDGE_DEV), jax.random.fold_in(splits[5], 1), 0, EDGE_DEV - 1).astype(jnp.int32),
        "trip_basis": noise(splits[6], (TRIPS, DT), 1.0, 6.0, ((0, 256),)),
        "edge_count": draw_edge_count(jax.random.fold_in(splits[14], 71), 0),
        "trip_count": draw_trip_count(jax.random.fold_in(splits[14], 71), 0),
        "w_a": noise(splits[9], (DA, DE), DA ** -0.5, 0.25),
        "w_down": noise(splits[10], (DE, DT), DE ** -0.5, 0.25),
        "w_t": noise(splits[11], (DT, DE), DT ** -0.5, 0.75),
        "w_b": noise(splits[12], (DE, DA), DE ** -0.5, 0.25),
        "cotangent": noise(splits[13], (ATOMS, DA), 1.0, 6.0, ((0, 256),)),
    }


def edge_pass(table_rows, edge_feats, sources, trip_src, trip_dst, basis, edge_valid, trip_valid, w_down, w_up):
    slots = sources.shape[0]
    edge_mask = (jnp.arange(slots) < edge_valid).astype(jnp.float32)[:, None]
    trip_mask = (jnp.arange(trip_src.shape[0]) < trip_valid).astype(jnp.float32)[:, None]
    incoming = edge_mask * (table_rows[sources].astype(jnp.float32) + edge_feats.astype(jnp.float32))
    down = jnp.dot(incoming, w_down.astype(jnp.float32), precision=lax.Precision.HIGHEST)
    trip_weight = basis.astype(jnp.float32) * trip_mask
    summed = jax.ops.segment_sum(trip_weight * down[trip_src], trip_dst, num_segments=slots).astype(jnp.bfloat16)
    preact = incoming + jnp.dot(summed, w_up, preferred_element_type=jnp.float32)
    outgoing = edge_mask * jax.nn.silu(preact)
    return (edge_mask, trip_weight, incoming, summed, preact, outgoing)

def edge_back(edge_mask, trip_weight, incoming, summed, preact, atom_grad, targets, sources, trip_src, trip_dst, w_down, w_up, table_len):
    slots = sources.shape[0]
    sigma = jax.nn.sigmoid(preact)
    dpre = edge_mask * atom_grad[targets] * sigma * (1.0 + preact * (1.0 - sigma))
    dsum = jnp.dot(dpre, w_up.astype(jnp.float32).T, precision=lax.Precision.HIGHEST)
    grad_up = jnp.dot(summed.astype(jnp.float32).T, dpre, precision=lax.Precision.HIGHEST)
    ddown = jax.ops.segment_sum(trip_weight * dsum[trip_dst], trip_src, num_segments=slots)
    grad_down = jnp.dot(incoming.T, ddown, precision=lax.Precision.HIGHEST)
    dincoming = edge_mask * (dpre + jnp.dot(ddown, w_down.astype(jnp.float32).T, precision=lax.Precision.HIGHEST))
    dtable = jax.ops.segment_sum(dincoming, sources, num_segments=table_len)
    return (dtable, grad_down, grad_up)

def per_device(array):
    return array.reshape((N_DOM, N_GP, -1) + array.shape[1:])

def reference(atoms, messages, edge_src, edge_dst, trip_in, trip_out, trip_basis, edge_count, trip_count, w_a, w_down, w_t, w_b, cotangent):
    proj = jnp.dot(atoms, w_a, preferred_element_type=jnp.float32).astype(jnp.bfloat16)
    blocks = proj.reshape(N_DOM, N_GP, ATOM_DEV, DE)
    tails = blocks[:, :, ATOM_DEV - GH:].reshape(N_DOM, N_GP * GH, DE)
    heads = blocks[:, :, :GH].reshape(N_DOM, N_GP * GH, DE)
    table = jnp.concatenate([jnp.roll(tails, 1, 0), blocks.reshape(N_DOM, A_DOM, DE), jnp.roll(heads, -1, 0)], 1)
    edge_counts = edge_count.reshape(N_DOM, N_GP)
    trip_counts = trip_count.reshape(N_DOM, N_GP)
    items = (table, per_device(messages), per_device(edge_src), per_device(edge_dst), per_device(trip_in), per_device(trip_out), per_device(trip_basis), edge_counts, trip_counts)

    def forward_slab(item):
        table_rows, feats, sources, targets, trip_src, trip_dst, basis, e_valid, t_valid = item
        total = jnp.zeros((A_DOM, DE), jnp.float32)
        for slot in range(N_GP):
            outs = edge_pass(table_rows, feats[slot], sources[slot], trip_src[slot], trip_dst[slot], basis[slot], e_valid[slot], t_valid[slot], w_down, w_t)
            total = total + jax.ops.segment_sum(outs[5], targets[slot], num_segments=A_DOM)
        return total
    atom_sum = lax.map(forward_slab, items).reshape(ATOMS, DE)
    atom_grad = jnp.dot(cotangent, w_b.T, preferred_element_type=jnp.float32)
    slab_grads = atom_grad.reshape(N_DOM, A_DOM, DE)

    def backward_slab(item):
        (table_rows, feats, sources, targets, trip_src, trip_dst, basis, e_valid, t_valid), slab_grad = item
        dtable_sum = jnp.zeros((A_EXT, DE), jnp.float32)
        down_sum = jnp.zeros((DE, DT), jnp.float32)
        up_sum = jnp.zeros((DT, DE), jnp.float32)
        for slot in range(N_GP):
            edge_mask, trip_weight, incoming, summed, preact, outgoing = edge_pass(table_rows, feats[slot], sources[slot], trip_src[slot], trip_dst[slot], basis[slot], e_valid[slot], t_valid[slot], w_down, w_t)
            dtable, grad_down, grad_up = edge_back(edge_mask, trip_weight, incoming, summed, preact, slab_grad, targets[slot], sources[slot], trip_src[slot], trip_dst[slot], w_down, w_t, A_EXT)
            dtable_sum = dtable_sum + dtable
            down_sum = down_sum + grad_down
            up_sum = up_sum + grad_up
        return (dtable_sum, down_sum, up_sum)
    dtables, down_terms, up_terms = lax.map(backward_slab, (items, slab_grads))
    rim = N_GP * GH
    lower_part = dtables[:, :rim]
    middle = dtables[:, rim:rim + A_DOM].reshape(N_DOM, N_GP, ATOM_DEV, DE)
    upper_part = dtables[:, rim + A_DOM:]
    to_tails = jnp.roll(lower_part, -1, 0).reshape(N_DOM, N_GP, GH, DE)
    to_heads = jnp.roll(upper_part, 1, 0).reshape(N_DOM, N_GP, GH, DE)
    middle = middle.at[:, :, ATOM_DEV - GH:].add(to_tails).at[:, :, :GH].add(to_heads)
    dproj = middle.reshape(ATOMS, DE)
    grad_atoms = jnp.dot(dproj, w_a.astype(jnp.float32).T, precision=lax.Precision.HIGHEST).astype(jnp.bfloat16)
    factor = 1.0 / math.sqrt(ATOMS)
    grad_wa = jnp.dot(atoms.astype(jnp.float32).T, dproj, precision=lax.Precision.HIGHEST) * factor
    grad_wd = lax.optimization_barrier(jnp.sum(down_terms, 0)) * factor
    grad_wt = lax.optimization_barrier(jnp.sum(up_terms, 0)) * factor
    grad_wb = jnp.dot(atom_sum.T, cotangent.astype(jnp.float32), precision=lax.Precision.HIGHEST) * factor
    return (grad_atoms, grad_wa, grad_wd, grad_wt, grad_wb)
```

```python
import functools
import math

import jax
import jax.numpy as jnp
from jax import lax
from jax.experimental import pallas as pl
from jax.experimental.pallas import tpu as pltpu
from jax.sharding import PartitionSpec as P

BF = jnp.bfloat16
F32 = jnp.float32
MESH = pl.DeviceIdType.MESH
GH = 128
OWN = 256
ROWS = 512
SLOTS = 2048
WIDTH = 512
DT = 64
LO = 256
BLK = 512
PIECE = 144


def dims_of(slabs):
    return {64: (4, 4, 4), 4: (1, 1, 4), 2: (1, 1, 2)}[slabs]


def nn(a, b):
    return lax.dot_general(a, b, (((1,), (0,)), ((), ())), preferred_element_type=F32)


def nt(a, b):
    return lax.dot_general(a, b, (((1,), (1,)), ((), ())), preferred_element_type=F32)


def tn(a, b):
    return lax.dot_general(a, b, (((0,), (0,)), ((), ())), preferred_element_type=F32)


def lanes(shape):
    return lax.broadcasted_iota(jnp.int32, shape, len(shape) - 1)


def pick_columns(index, first, width):
    lane = lanes(index.shape)
    local = index - first
    return jnp.concatenate(
        [jnp.where(local == lane + 128 * j, 1.0, 0.0).astype(BF) for j in range(width // 128)], axis=1
    )


def pick_rows(index, first, height):
    shape = (height, index.shape[1])
    row = lax.broadcasted_iota(jnp.int32, shape, 0)
    return jnp.where(row == jnp.broadcast_to(index - first, shape), 1.0, 0.0).astype(BF)


def table_row(src):
    lower = ((src >> 7) << 9) + (src & 127)
    mid = src - 512
    middle = ((mid >> 8) << 9) + GH + (mid & 255)
    up = src - 1536
    upper = ((up >> 7) << 9) + GH + OWN + (up & 127)
    return jnp.where(src < 512, lower, jnp.where(src < 1536, middle, upper))


def kernel(
    dims,
    ecnt_ref, tcnt_ref, src_ref, dst_ref, tin_ref, tout_ref,
    atoms_ref, cot_ref, msg_hbm, basis_ref, wa_ref, wdown_ref, wt_ref, wb_ref,
    full_out, grad_out,
    table, cots, msg, picked, inc, dpre, dinc, dtable, rd, ed, re, own_sum, rims_in, rims_out,
    src_col, dst_col, tin_col, tout_col, rows, basis2, wdown2, wt2,
    down, dn, acc_s, sm,
    acc_wa, acc_wb, acc_wt, acc_wd, pieces, rc, half, rx, zbuf, rz_main, rz_small, full,
    send, recv, local_sem,
):
    Y, ZH, X = dims
    XY = X * Y
    Z = 2 * ZH
    nb = 16 // XY
    tile = 128 // Z
    dom = lax.axis_index("dom")
    gp = lax.axis_index("gp")
    slabs = Y * ZH * X
    x = lax.rem(dom, X)
    zh = lax.rem(lax.div(dom, X), ZH)
    y = lax.div(dom, X * ZH)
    core = lax.rem(gp, 2)
    zl = lax.div(gp, 2)
    z = zh * 2 + zl

    sib = {"dom": dom, "gp": zl * 2 + (1 - core)}
    zpart = {"dom": dom, "gp": (1 - zl) * 2 + core}
    kz = (1 - zl) * 2 + core
    above = {"dom": lax.rem(dom + 1, slabs), "gp": gp}
    below = {"dom": lax.rem(dom + slabs - 1, slabs), "gp": gp}
    xy_peers = []
    for j in range(1, XY):
        px = lax.rem(x + j // Y, X)
        py = lax.rem(y + j % Y, Y)
        xy_peers.append((px * Y + py, {"dom": (py * ZH + zh) * X + px, "gp": gp}))
    z_peers = []
    for j in range(1, Z):
        pz = lax.rem(z + j, Z)
        z_peers.append((pz, {"dom": (y * ZH + lax.div(pz, 2)) * X + x, "gp": lax.rem(pz, 2) * 2 + core}))

    barrier = pltpu.get_barrier_semaphore()
    others = [sib, above, below] + [d for _, d in xy_peers] + [d for _, d in z_peers]
    for d in others:
        pl.semaphore_signal(barrier, inc=1, device_id=d, device_id_type=MESH)

    count = [0]
    started = []

    def remote(src, dst, device):
        i = count[0]
        count[0] += 1
        c = pltpu.make_async_remote_copy(
            src_ref=src, dst_ref=dst, send_sem=send.at[i], recv_sem=recv.at[i],
            device_id=device, device_id_type=MESH,
        )
        c.start()
        started.append(c)
        return c

    msg_copy = pltpu.make_async_copy(msg_hbm, msg, local_sem.at[0])
    msg_copy.start()
    pl.semaphore_wait(barrier, len(others))

    mid = pl.ds(GH, OWN)
    low = pl.ds(0, GH)
    high = pl.ds(GH + OWN, GH)
    to_z = remote(atoms_ref, table.at[gp, mid], zpart)
    to_above = remote(atoms_ref.at[pl.ds(OWN - GH, GH)], table.at[gp, low], above)
    to_below = remote(atoms_ref.at[pl.ds(0, GH)], table.at[gp, high], below)
    to_sib = remote(atoms_ref, table.at[gp, mid], sib)
    table[gp, mid] = atoms_ref[...]
    cots[gp] = cot_ref[...]

    edges = ecnt_ref[0]
    trips = tcnt_ref[0]
    for n, (ref, col) in enumerate(
        ((src_ref, src_col), (dst_ref, dst_col), (tin_ref, tin_col), (tout_ref, tout_col))
    ):
        flat = ref[...]
        if n == 0:
            flat = table_row(flat)
        for j in range(SLOTS // 128):
            line = flat[j : j + 1]
            rows[n : n + 1, 128 * j : 128 * (j + 1)] = line
            col[128 * j : 128 * (j + 1)] = jnp.transpose(jnp.broadcast_to(line, (128, 128)))
    twice = jnp.where(
        lax.broadcasted_iota(jnp.int32, (DT, 128), 0) == (lanes((DT, 128)) & (DT - 1)), 1.0, 0.0
    ).astype(BF)
    valid = lax.broadcasted_iota(jnp.int32, (SLOTS, 128), 0) < trips
    basis2[...] = jnp.where(valid, nn(basis_ref[...], twice), 0.0)
    wdown2[...] = nn(wdown_ref[...], twice).astype(BF)
    wt2[...] = jnp.concatenate([wt_ref[...], wt_ref[...]], axis=0)

    to_above.wait_recv()
    z_low = remote(table.at[gp, low], table.at[gp, low], zpart)
    s_low = remote(table.at[gp, low], table.at[gp, low], sib)
    to_below.wait_recv()
    z_high = remote(table.at[gp, high], table.at[gp, high], zpart)
    s_high = remote(table.at[gp, high], table.at[gp, high], sib)
    z_cot = remote(cot_ref, cots.at[gp], zpart)
    s_cot = remote(cot_ref, cots.at[gp], sib)
    to_z.wait_recv()
    f_mid = remote(table.at[kz, mid], table.at[kz, mid], sib)
    z_low.wait_recv()
    f_low = remote(table.at[kz, low], table.at[kz, low], sib)
    z_high.wait_recv()
    f_high = remote(table.at[kz, high], table.at[kz, high], sib)
    msg_copy.wait()
    for c in (to_sib, s_low, s_high, f_mid, f_low, f_high):
        c.wait_recv()

    def row_mask(start, n, width):
        return lax.broadcasted_iota(jnp.int32, (n, width), 0) + start < edges

    def edge_in(b, carry):
        at = pl.ds(pl.multiple_of(b * BLK, BLK), BLK)
        index = src_col[at]
        got = nn(pick_columns(index, 0, ROWS), table[0])
        for k in range(1, 4):
            got = got + nn(pick_columns(index, k * ROWS, ROWS), table[k])
        got = got.astype(BF)
        picked[at] = got
        proj = nn(got, wa_ref[...]).astype(BF).astype(F32)
        value = jnp.where(row_mask(b * BLK, BLK, WIDTH), proj + msg[at].astype(F32), 0.0)
        inc[at] = value
        down[at] = nn(value.astype(BF), wdown2[...]).astype(BF)
        return carry

    lax.fori_loop(0, SLOTS // BLK, edge_in, 0)
    z_cot.wait_recv()
    f_cot = remote(cots.at[kz], cots.at[kz], sib)

    def pack(source):
        first = lanes((LO, 128)) < DT
        for j in range(4):
            a = source[2 * j * LO : (2 * j + 1) * LO].astype(F32)
            b = source[(2 * j + 1) * LO : (2 * j + 2) * LO].astype(F32)
            dn[:, 128 * j : 128 * (j + 1)] = jnp.where(first, a, b).astype(BF)

    def unpack():
        first = lanes((LO, 128)) < DT
        for j in range(4):
            v = acc_s[:, 128 * j : 128 * (j + 1)]
            sm[2 * j * LO : (2 * j + 1) * LO] = jnp.where(first, v, 0.0).astype(BF)
            sm[(2 * j + 1) * LO : (2 * j + 2) * LO] = jnp.where(first, 0.0, v).astype(BF)

    def triplets(from_col, to_col, to_row):
        half_lane = jnp.where(lanes((BLK, 128)) < DT, 0, 1)
        acc_s[...] = jnp.zeros_like(acc_s)

        def body(b, carry):
            at = pl.ds(pl.multiple_of(b * BLK, BLK), BLK)
            frm = from_col[at]
            to = to_col[at]
            got = nn(pick_columns(frm & (LO - 1), 0, LO), dn[...])
            frm_hi = frm >> 8
            to_hi = to >> 8
            value = jnp.where(frm_hi == half_lane, got[:, 0:128], 0.0)
            for j in range(1, 4):
                value = value + jnp.where(
                    frm_hi == half_lane + 2 * j, got[:, 128 * j : 128 * (j + 1)], 0.0
                )
            value = value + pltpu.roll(value, DT, 1)
            value = value * basis2[at]
            spread = jnp.concatenate(
                [jnp.where(to_hi == half_lane + 2 * j, value, 0.0).astype(BF) for j in range(4)], axis=1
            )
            line = rows[to_row : to_row + 1, pl.ds(pl.multiple_of(b * BLK, BLK), BLK)]
            acc_s[...] += nn(pick_rows(line & (LO - 1), 0, LO), spread)
            return carry

        lax.fori_loop(0, SLOTS // BLK, body, 0)

    pack(down)
    triplets(tin_col, tout_col, 3)
    unpack()
    s_cot.wait_recv()
    f_cot.wait_recv()

    acc_wb[...] = jnp.zeros_like(acc_wb)
    acc_wt[...] = jnp.zeros_like(acc_wt)

    def edge_mid(b, carry):
        at = pl.ds(pl.multiple_of(b * BLK, BLK), BLK)
        mask = row_mask(b * BLK, BLK, WIDTH)
        index = dst_col[at]
        cot = nn(pick_columns(index, 0, OWN), cots[0])
        for k in range(1, 4):
            cot = cot + nn(pick_columns(index, k * OWN, OWN), cots[k])
        cot = cot.astype(BF)
        atom_grad = nt(cot, wb_ref[...])
        summed = sm[at]
        pre = inc[at] + nn(summed, wt2[...])
        sig = jax.nn.sigmoid(pre)
        out = jnp.where(mask, pre * sig, 0.0).astype(BF)
        grad = jnp.where(mask, atom_grad * sig * (1.0 + pre * (1.0 - sig)), 0.0)
        dpre[at] = grad
        grad = grad.astype(BF)
        acc_wb[...] += tn(out, cot)
        acc_wt[...] += tn(summed, grad)
        down[at] = nt(grad, wt2[...]).astype(BF)
        return carry

    lax.fori_loop(0, SLOTS // BLK, edge_mid, 0)

    pack(down)
    triplets(tout_col, tin_col, 2)
    unpack()

    acc_wa[...] = jnp.zeros_like(acc_wa)
    acc_wd[...] = jnp.zeros_like(acc_wd)

    def edge_out(b, carry):
        at = pl.ds(pl.multiple_of(b * BLK, BLK), BLK)
        mask = row_mask(b * BLK, BLK, WIDTH)
        back = sm[at]
        grad = jnp.where(mask, dpre[at] + nt(back, wdown2[...]), 0.0).astype(BF)
        dinc[at] = grad
        acc_wd[...] += tn(back, inc[at].astype(BF))
        acc_wa[...] += tn(picked[at], grad)
        return carry

    lax.fori_loop(0, SLOTS // BLK, edge_out, 0)

    for s in range(32):
        big, small = (acc_wa, acc_wt) if s < 16 else (acc_wb, acc_wd)
        r, c = (s % 16) // 4, s % 4
        cols = slice(128 * c, 128 * (c + 1))
        pieces[s, 0:128] = big[128 * r : 128 * (r + 1), cols].astype(BF)
        pieces[s, 128:144] = (
            small[16 * r : 16 * (r + 1), cols] + small[DT + 16 * r : DT + 16 * (r + 1), cols]
        ).astype(BF)
    w_core = remote(pieces.at[pl.ds((1 - core) * 16, 16)], rc, sib)

    def table_grad(k):
        total = nn(pick_rows(rows[0:1, 0:BLK], k * ROWS, ROWS), dinc[0:BLK])
        for b in range(1, SLOTS // BLK):
            part = slice(BLK * b, BLK * (b + 1))
            total = total + nn(pick_rows(rows[0:1, part], k * ROWS, ROWS), dinc[part])
        dtable[k] = total.astype(BF)

    table_grad(1 - core)
    d_core0 = remote(dtable.at[1 - core], rd.at[0], sib)
    table_grad(3 - core)
    d_core1 = remote(dtable.at[3 - core], rd.at[1], sib)

    w_core.wait_recv()
    mine = pieces[pl.ds(core * 16, 16)].astype(F32) + rc[...].astype(F32)
    half[...] = mine.astype(BF)
    w_xy = [
        remote(half.at[pl.ds(s * nb, nb)], rx.at[j], d) for j, (s, d) in enumerate(xy_peers)
    ]

    def table_grads(i, carry):
        table_grad(2 * i + core)
        return carry

    lax.fori_loop(0, 2, table_grads, 0)
    d_core0.wait_recv()
    d_core1.wait_recv()
    ed[...] = (dtable[kz].astype(F32) + rd[1 - zl].astype(F32)).astype(BF)
    d_z = remote(ed, re, zpart)
    own_sum[...] = dtable[gp].astype(F32) + rd[zl].astype(F32)

    for c in w_xy:
        c.wait_recv()
    own_s = x * Y + y
    total = half[pl.ds(own_s * nb, nb)].astype(F32)
    for j in range(XY - 1):
        total = total + rx[j].astype(F32)
    zbuf[...] = total.astype(BF)
    w_z = []
    for j, (pz, d) in enumerate(z_peers):
        part = pl.ds(pl.multiple_of(pz * tile, tile), tile)
        w_z.append(remote(zbuf.at[:, part], rz_main.at[j + 1], d))
        w_z.append(remote(zbuf.at[:, pl.ds(128, 16)], rz_small.at[j + 1], d))
    own_rows = pl.ds(pl.multiple_of(z * tile, tile), tile)
    rz_small[0] = zbuf[:, 128:144]

    d_z.wait_recv()
    summed_table = own_sum[...] + re[...].astype(F32)
    own_sum[...] = summed_table
    rims_out[0] = summed_table[0:GH].astype(BF)
    rims_out[1] = summed_table[GH + OWN :].astype(BF)
    to_tails = remote(rims_out.at[0], rims_in.at[0], below)
    to_heads = remote(rims_out.at[1], rims_in.at[1], above)

    for c in w_z:
        c.wait_recv()
    total = zbuf[:, own_rows].astype(F32)
    for j in range(1, Z):
        total = total + rz_main[j].astype(F32)
    small = rz_small[lax.rem(Z - z, Z)].astype(F32)
    for j in range(1, Z):
        small = small + rz_small[lax.rem(j + Z - z, Z)].astype(F32)
    own_piece = pl.ds(core * 16 + own_s * nb, nb)
    full[own_piece, own_rows] = total.astype(BF)
    full[own_piece, 128:144] = small.astype(BF)
    g_z = [
        remote(full.at[own_piece, own_rows], full.at[own_piece, own_rows], d) for _, d in z_peers
    ]

    to_tails.wait_recv()
    to_heads.wait_recv()
    dproj = own_sum[GH : GH + OWN] + jnp.concatenate(
        [rims_in[1].astype(F32), rims_in[0].astype(F32)], axis=0
    )
    coarse = dproj.astype(BF)
    fine = (dproj - coarse.astype(F32)).astype(BF)
    grad_out[...] = (nt(coarse, wa_ref[...]) + nt(fine, wa_ref[...])).astype(BF)

    for c in g_z:
        c.wait_recv()
    g_xy = [remote(full.at[own_piece], full.at[own_piece], d) for _, d in xy_peers]
    for c in g_xy:
        c.wait_recv()
    own_core = pl.ds(core * 16, 16)
    g_core = remote(full.at[own_core], full.at[own_core], sib)
    g_core.wait_recv()
    full_out[...] = full[...]
    for c in started:
        c.wait_send()


def finish(factor, full_ref, grad_ref, gatoms_ref, gwa_ref, gwd_ref, gwt_ref, gwb_ref):
    gatoms_ref[...] = grad_ref[...]
    down_rows = []
    for r in range(4):
        for c in range(4):
            s = 4 * r + c
            cols = slice(128 * c, 128 * (c + 1))
            gwa_ref[128 * r : 128 * (r + 1), cols] = full_ref[s, 0:128].astype(F32) * factor
            gwb_ref[128 * r : 128 * (r + 1), cols] = full_ref[s + 16, 0:128].astype(F32) * factor
            gwt_ref[16 * r : 16 * (r + 1), cols] = full_ref[s, 128:144].astype(F32) * factor
    for c in range(4):
        stack = jnp.concatenate(
            [full_ref[16 + 4 * r + c, 128:144].astype(F32) * factor for r in range(4)] * 2, axis=0
        )
        gwd_ref[128 * c : 128 * (c + 1)] = jnp.transpose(stack)[:, 0:DT]


def per_device(
    slabs, groups,
    atoms, messages, edge_src, edge_dst, trip_in, trip_out, trip_basis, edge_count, trip_count,
    w_a, w_down, w_t, w_b, cotangent,
):
    dims = dims_of(slabs)
    Y, ZH, X = dims
    XY, Z = X * Y, 2 * ZH
    nb, tile = 16 // XY, 128 // Z
    transfers = 3 + 1 + 6 + 3 + 1 + 3 + 1 + 2 + 2 * (XY - 1) + 3 * (Z - 1) + 8
    vmem = pl.BlockSpec(memory_space=pltpu.VMEM)
    smem = pl.BlockSpec(memory_space=pltpu.SMEM)
    hbm = pl.BlockSpec(memory_space=pl.ANY)
    index = [a.reshape(16, 128) for a in (edge_src, edge_dst, trip_in, trip_out)]
    V = pltpu.VMEM
    full, grad = pl.pallas_call(
        functools.partial(kernel, dims),
        out_shape=(
            jax.ShapeDtypeStruct((32, PIECE, 128), BF),
            jax.ShapeDtypeStruct((OWN, WIDTH), BF),
        ),
        in_specs=[smem, smem] + [vmem] * 6 + [hbm] + [vmem] * 5,
        out_specs=(vmem, vmem),
        scratch_shapes=[
            V((4, ROWS, WIDTH), BF), V((4, OWN, WIDTH), BF), V((SLOTS, WIDTH), BF),
            V((SLOTS, WIDTH), BF), V((SLOTS, WIDTH), F32), V((SLOTS, WIDTH), F32),
            V((SLOTS, WIDTH), BF), V((4, ROWS, WIDTH), BF), V((2, ROWS, WIDTH), BF),
            V((ROWS, WIDTH), BF), V((ROWS, WIDTH), BF), V((ROWS, WIDTH), F32),
            V((2, GH, WIDTH), BF), V((2, GH, WIDTH), BF),
            V((SLOTS, 128), jnp.int32), V((SLOTS, 128), jnp.int32),
            V((SLOTS, 128), jnp.int32), V((SLOTS, 128), jnp.int32),
            V((8, SLOTS), jnp.int32), V((SLOTS, 128), F32), V((WIDTH, 128), BF), V((128, WIDTH), BF),
            V((SLOTS, 128), BF), V((LO, WIDTH), BF), V((LO, WIDTH), F32), V((SLOTS, 128), BF),
            V((512, WIDTH), F32), V((512, WIDTH), F32), V((128, WIDTH), F32), V((128, WIDTH), F32),
            V((32, PIECE, 128), BF), V((16, PIECE, 128), BF), V((16, PIECE, 128), BF),
            V((XY - 1, nb, PIECE, 128), BF), V((nb, PIECE, 128), BF),
            V((Z, nb, tile, 128), BF), V((Z, nb, 16, 128), BF), V((32, PIECE, 128), BF),
            pltpu.SemaphoreType.DMA((transfers,)), pltpu.SemaphoreType.DMA((transfers,)),
            pltpu.SemaphoreType.DMA((1,)),
        ],
        compiler_params=pltpu.CompilerParams(
            collective_id=0, has_side_effects=True, vmem_limit_bytes=60 * 1024 * 1024
        ),
    )(
        edge_count, trip_count, *index, atoms, cotangent, messages, trip_basis, w_a, w_down, w_t, w_b
    )
    factor = 1.0 / math.sqrt(OWN * groups * slabs)
    return pl.pallas_call(
        functools.partial(finish, factor),
        out_shape=(
            jax.ShapeDtypeStruct((OWN, WIDTH), BF),
            jax.ShapeDtypeStruct((512, WIDTH), F32),
            jax.ShapeDtypeStruct((WIDTH, DT), F32),
            jax.ShapeDtypeStruct((DT, WIDTH), F32),
            jax.ShapeDtypeStruct((512, WIDTH), F32),
        ),
        in_specs=[vmem, vmem],
        out_specs=(vmem,) * 5,
        compiler_params=pltpu.CompilerParams(vmem_limit_bytes=32 * 1024 * 1024),
    )(full, grad)


def solution(mesh):
    both = P(("dom", "gp"))
    rows = P(("dom", "gp"), None)
    in_specs = (rows, rows, both, both, both, both, rows, both, both, P(), P(), P(), P(), rows)
    out_specs = (rows, P(), P(), P(), P())
    return jax.shard_map(
        functools.partial(per_device, mesh.shape["dom"], mesh.shape["gp"]),
        mesh=mesh, in_specs=in_specs, out_specs=out_specs, check_vma=False,
    )
```

```python
import functools
import math

import jax
import jax.numpy as jnp
from jax import lax
from jax.experimental import pallas as pl
from jax.experimental.pallas import tpu as pltpu
from jax.sharding import PartitionSpec as P

BF = jnp.bfloat16
F32 = jnp.float32
MESH = pl.DeviceIdType.MESH
GH = 128
OWN = 256
ROWS = 512
SLOTS = 2048
WIDTH = 512
DT = 64
LO = 256
BLK = 512


def dims_of(slabs):
    return {64: (4, 4, 4), 4: (1, 1, 4), 2: (1, 1, 2)}[slabs]


def nn(a, b):
    return lax.dot_general(a, b, (((1,), (0,)), ((), ())), preferred_element_type=F32)


def nt(a, b):
    return lax.dot_general(a, b, (((1,), (1,)), ((), ())), preferred_element_type=F32)


def tn(a, b):
    return lax.dot_general(a, b, (((0,), (0,)), ((), ())), preferred_element_type=F32)


def lanes(shape):
    return lax.broadcasted_iota(jnp.int32, shape, len(shape) - 1)


def pick_columns(index, first, width):
    lane = lanes(index.shape)
    local = index - first
    return jnp.concatenate(
        [jnp.where(local == lane + 128 * j, 1.0, 0.0).astype(BF) for j in range(width // 128)], axis=1
    )


def pick_rows(index, first, height):
    shape = (height, index.shape[1])
    row = lax.broadcasted_iota(jnp.int32, shape, 0)
    return jnp.where(row == jnp.broadcast_to(index - first, shape), 1.0, 0.0).astype(BF)


def table_row(src):
    up = src - 1536
    lower = 4 * OWN + ((src >> 7) << 8) + (src & 127)
    upper = 4 * OWN + ((up >> 7) << 8) + GH + (up & 127)
    return jnp.where(src < 512, lower, jnp.where(src < 1536, src - 512, upper))


def kernel(
    dims,
    ecnt_ref, tcnt_ref, src_ref, dst_ref, tin_ref, tout_ref, wdown_ref, wt_ref,
    atoms_hbm, cot_hbm, msg_hbm, basis_hbm, wa_hbm, wb_hbm,
    full_out, grad_out,
    mid, rim, cots, msg, basis, wa, wb, picked, inc, dpre,
    src_col, dst_col, tin_col, tout_col, rows, basis2, wdown2, wt2,
    down, dn, acc_s, sm,
    dt, rd, ed, re, own_sum, dt2, rd2, ed2, re2, rims_out, rims_in, rims2_out, rims2_in,
    acc_wa, acc_wb, acc_wt, acc_wd, acc_wx, pieces, rc, half, rx, late, rc2, half2, rx2,
    zbuf, rz_main, rz_small, full,
    send, recv, local_sem,
):
    Y, ZH, X = dims
    XY = X * Y
    Z = 2 * ZH
    nb = 16 // XY
    tile = 128 // Z
    dom = lax.axis_index("dom")
    gp = lax.axis_index("gp")
    slabs = Y * ZH * X
    x = lax.rem(dom, X)
    zh = lax.rem(lax.div(dom, X), ZH)
    y = lax.div(dom, X * ZH)
    core = lax.rem(gp, 2)
    zl = lax.div(gp, 2)
    z = zh * 2 + zl

    sib = {"dom": dom, "gp": zl * 2 + (1 - core)}
    zpart = {"dom": dom, "gp": (1 - zl) * 2 + core}
    kz = (1 - zl) * 2 + core
    above = {"dom": lax.rem(dom + 1, slabs), "gp": gp}
    below = {"dom": lax.rem(dom + slabs - 1, slabs), "gp": gp}
    xy_peers = []
    for j in range(1, XY):
        px = lax.rem(x + j // Y, X)
        py = lax.rem(y + j % Y, Y)
        xy_peers.append((px * Y + py, {"dom": (py * ZH + zh) * X + px, "gp": gp}))
    z_peers = []
    for j in range(1, Z):
        pz = lax.rem(z + j, Z)
        z_peers.append((pz, {"dom": (y * ZH + lax.div(pz, 2)) * X + x, "gp": lax.rem(pz, 2) * 2 + core}))

    barrier = pltpu.get_barrier_semaphore()
    others = [sib, above, below] + [d for _, d in xy_peers] + [d for _, d in z_peers]
    for d in others:
        pl.semaphore_signal(barrier, inc=1, device_id=d, device_id_type=MESH)

    count = [0]
    started = []

    def remote(src, dst, device):
        i = count[0]
        count[0] += 1
        c = pltpu.make_async_remote_copy(
            src_ref=src, dst_ref=dst, send_sem=send.at[i], recv_sem=recv.at[i],
            device_id=device, device_id_type=MESH,
        )
        c.start()
        started.append(c)
        return c

    local = []
    for i, (src, dst) in enumerate(
        (
            (atoms_hbm, mid.at[gp]), (cot_hbm, cots.at[gp]), (basis_hbm, basis),
            (wa_hbm, wa), (msg_hbm, msg), (wb_hbm, wb),
        )
    ):
        c = pltpu.make_async_copy(src, dst, local_sem.at[i])
        c.start()
        local.append(c)
    atoms_in, cot_in, basis_in, wa_in, msg_in, wb_in = local

    pl.semaphore_wait(barrier, len(others))

    low = pl.ds(0, GH)
    high = pl.ds(GH, GH)
    to_above = remote(atoms_hbm.at[high], rim.at[gp, low], above)
    to_below = remote(atoms_hbm.at[low], rim.at[gp, high], below)
    to_z = remote(atoms_hbm, mid.at[gp], zpart)
    to_sib = remote(atoms_hbm, mid.at[gp], sib)

    edges = ecnt_ref[0]
    trips = tcnt_ref[0]
    for n, (ref, col) in enumerate(
        ((src_ref, src_col), (dst_ref, dst_col), (tin_ref, tin_col), (tout_ref, tout_col))
    ):
        flat = ref[...]
        if n == 0:
            flat = table_row(flat)
        for j in range(SLOTS // 128):
            line = flat[j : j + 1]
            rows[n : n + 1, 128 * j : 128 * (j + 1)] = line
            col[128 * j : 128 * (j + 1)] = jnp.transpose(jnp.broadcast_to(line, (128, 128)))
    wdown2[...] = jnp.concatenate([wdown_ref[...], wdown_ref[...]], axis=0)
    wt2[...] = jnp.concatenate([wt_ref[...], wt_ref[...]], axis=0)
    basis_in.wait()
    twice = jnp.where(
        lax.broadcasted_iota(jnp.int32, (DT, 128), 0) == (lanes((DT, 128)) & (DT - 1)), 1.0, 0.0
    ).astype(BF)
    valid = lax.broadcasted_iota(jnp.int32, (SLOTS, 128), 0) < trips
    basis2[...] = jnp.where(valid, tn(basis[...], twice), 0.0)

    atoms_in.wait()
    to_sib.wait_recv()
    to_above.wait_recv()
    z_low = remote(rim.at[gp, low], rim.at[gp, low], zpart)
    s_low = remote(rim.at[gp, low], rim.at[gp, low], sib)
    to_below.wait_recv()
    z_high = remote(rim.at[gp, high], rim.at[gp, high], zpart)
    s_high = remote(rim.at[gp, high], rim.at[gp, high], sib)
    z_cot = remote(cot_hbm, cots.at[gp], zpart)
    s_cot = remote(cot_hbm, cots.at[gp], sib)
    to_z.wait_recv()
    f_mid = remote(mid.at[kz], mid.at[kz], sib)
    f_mid.wait_recv()

    def block(b):
        return pl.ds(pl.multiple_of(b * BLK, BLK), BLK)

    def gather(index, first, source):
        got = nn(pick_columns(index, first, OWN), source[0])
        for k in range(1, 4):
            got = got + nn(pick_columns(index, first + k * OWN, OWN), source[k])
        return got

    def edge_own(b, carry):
        picked[block(b)] = gather(src_col[block(b)], 0, mid).astype(BF)
        return carry

    lax.fori_loop(0, SLOTS // BLK, edge_own, 0)

    z_low.wait_recv()
    f_low = remote(rim.at[kz, low], rim.at[kz, low], sib)
    z_high.wait_recv()
    f_high = remote(rim.at[kz, high], rim.at[kz, high], sib)
    for c in (s_low, s_high, f_low, f_high):
        c.wait_recv()
    wa_in.wait()
    msg_in.wait()

    def row_mask(b, width):
        return lax.broadcasted_iota(jnp.int32, (BLK, width), 0) + b * BLK < edges

    def edge_in(b, carry):
        at = block(b)
        got = (picked[at].astype(F32) + gather(src_col[at], 4 * OWN, rim)).astype(BF)
        picked[at] = got
        proj = nn(got, wa[...]).astype(BF).astype(F32)
        value = jnp.where(row_mask(b, WIDTH), proj + msg[at].astype(F32), 0.0)
        inc[at] = value
        down[at] = nt(value.astype(BF), wdown2[...]).astype(BF)
        return carry

    lax.fori_loop(0, SLOTS // BLK, edge_in, 0)
    z_cot.wait_recv()
    f_cot = remote(cots.at[kz], cots.at[kz], sib)

    def pack(source):
        first = lanes((LO, 128)) < DT
        for j in range(4):
            a = source[2 * j * LO : (2 * j + 1) * LO].astype(F32)
            b = source[(2 * j + 1) * LO : (2 * j + 2) * LO].astype(F32)
            dn[:, 128 * j : 128 * (j + 1)] = jnp.where(first, a, b).astype(BF)

    def unpack():
        first = lanes((LO, 128)) < DT
        for j in range(4):
            v = acc_s[:, 128 * j : 128 * (j + 1)]
            sm[2 * j * LO : (2 * j + 1) * LO] = jnp.where(first, v, 0.0).astype(BF)
            sm[(2 * j + 1) * LO : (2 * j + 2) * LO] = jnp.where(first, 0.0, v).astype(BF)

    def triplets(from_col, to_col, to_row):
        half_lane = jnp.where(lanes((BLK, 128)) < DT, 0, 1)
        acc_s[...] = jnp.zeros_like(acc_s)

        def body(b, carry):
            at = block(b)
            frm = from_col[at]
            to = to_col[at]
            got = nn(pick_columns(frm & (LO - 1), 0, LO), dn[...])
            frm_hi = frm >> 8
            to_hi = to >> 8
            value = jnp.where(frm_hi == half_lane, got[:, 0:128], 0.0)
            for j in range(1, 4):
                value = value + jnp.where(
                    frm_hi == half_lane + 2 * j, got[:, 128 * j : 128 * (j + 1)], 0.0
                )
            value = value + pltpu.roll(value, DT, 1)
            value = value * basis2[at]
            spread = jnp.concatenate(
                [jnp.where(to_hi == half_lane + 2 * j, value, 0.0).astype(BF) for j in range(4)], axis=1
            )
            line = rows[to_row : to_row + 1, block(b)]
            acc_s[...] += nn(pick_rows(line & (LO - 1), 0, LO), spread)
            return carry

        lax.fori_loop(0, SLOTS // BLK, body, 0)

    pack(down)
    triplets(tin_col, tout_col, 3)
    unpack()
    cot_in.wait()
    wb_in.wait()
    s_cot.wait_recv()
    f_cot.wait_recv()

    for acc in (acc_wa, acc_wb, acc_wt, acc_wd, acc_wx):
        acc[...] = jnp.zeros_like(acc)

    def edge_mid(b, carry):
        at = block(b)
        mask = row_mask(b, WIDTH)
        cot = gather(dst_col[at], 0, cots).astype(BF)
        atom_grad = nt(cot, wb[...])
        summed = sm[at]
        pre = inc[at] + nn(summed, wt2[...])
        sig = jax.nn.sigmoid(pre)
        out = jnp.where(mask, pre * sig, 0.0).astype(BF)
        grad = jnp.where(mask, atom_grad * sig * (1.0 + pre * (1.0 - sig)), 0.0).astype(BF)
        dpre[at] = grad
        acc_wb[...] += tn(out, cot)
        acc_wa[...] += tn(picked[at], grad)
        acc_wt[...] += tn(summed, grad)
        down[at] = nt(grad, wt2[...]).astype(BF)
        return carry

    lax.fori_loop(0, SLOTS // BLK, edge_mid, 0)

    def fold(acc, r, cols):
        return (acc[16 * r : 16 * (r + 1), cols] + acc[DT + 16 * r : DT + 16 * (r + 1), cols]).astype(BF)

    for s in range(32):
        r, c = (s % 16) // 4, s % 4
        cols = slice(128 * c, 128 * (c + 1))
        pieces[s, 0:128] = (acc_wa if s < 16 else acc_wb)[128 * r : 128 * (r + 1), cols].astype(BF)
        pieces[s, 128:144] = fold(acc_wt, r, cols) if s < 16 else jnp.zeros((16, 128), BF)
    not_mine = pl.ds((1 - core) * 16, 16)
    mine = pl.ds(core * 16, 16)
    w_core = remote(pieces.at[not_mine], rc, sib)

    def table_grad(owner, source, out, who):
        for part in range(2):
            first = (4 + owner) * OWN if part == 0 else owner * OWN
            total = None
            for b in range(SLOTS // BLK):
                cols = slice(BLK * b, BLK * (b + 1))
                line = rows[0:1, cols]
                choice = jnp.concatenate(
                    [pick_rows(line, first, OWN), pick_rows(line, first + 2 * OWN, OWN)], axis=0
                )
                term = nn(choice, source[cols])
                total = term if total is None else total + term
            total = total.astype(BF)
            out[who, 0, OWN * part : OWN * (part + 1)] = total[0:OWN]
            out[who, 1, OWN * part : OWN * (part + 1)] = total[OWN:]

    table_grad(1 - core, dpre, dt, 0)
    d_core = remote(dt.at[0], rd, sib)
    w_core.wait_recv()
    half[...] = (pieces[mine].astype(F32) + rc[...].astype(F32)).astype(BF)
    w_xy = [
        remote(half.at[pl.ds(s * nb, nb)], rx.at[j], d) for j, (s, d) in enumerate(xy_peers)
    ]
    table_grad(core, dpre, dt, 1)
    d_core.wait_recv()
    ed[...] = (dt[1, 1 - zl].astype(F32) + rd[1 - zl].astype(F32)).astype(BF)
    rim_part = pl.ds(0, OWN)
    mid_part = pl.ds(OWN, OWN)
    d_rim = remote(ed.at[rim_part], re.at[rim_part], zpart)
    d_mid = remote(ed.at[mid_part], re.at[mid_part], zpart)

    pack(down)
    triplets(tout_col, tin_col, 2)
    unpack()

    def edge_out(b, carry):
        at = block(b)
        back = jnp.where(row_mask(b, 128), sm[at].astype(F32), 0.0).astype(BF)
        sm[at] = back
        acc_wd[...] += tn(back, inc[at].astype(BF))
        acc_wx[...] += tn(back, picked[at])
        return carry

    lax.fori_loop(0, SLOTS // BLK, edge_out, 0)
    for s in range(32):
        r, c = (s % 16) // 4, s % 4
        late[s] = fold(acc_wd if s < 16 else acc_wx, r, slice(128 * c, 128 * (c + 1)))
    l_core = remote(late.at[not_mine], rc2, sib)
    table_grad(1 - core, sm, dt2, 0)
    d2_core = remote(dt2.at[0], rd2, sib)
    l_core.wait_recv()
    half2[...] = (late[mine].astype(F32) + rc2[...].astype(F32)).astype(BF)
    l_xy = [
        remote(half2.at[pl.ds(s * nb, nb)], rx2.at[j], d) for j, (s, d) in enumerate(xy_peers)
    ]

    own_s = x * Y + y
    own_rows = pl.ds(pl.multiple_of(z * tile, tile), tile)
    own_piece = pl.ds(core * 16 + own_s * nb, nb)

    def sum_xy(copies, buffer, received):
        for c in copies:
            c.wait_recv()
        total = buffer[pl.ds(own_s * nb, nb)].astype(F32)
        for j in range(XY - 1):
            total = total + received[j].astype(F32)
        return total.astype(BF)

    zbuf[:, 0:144] = sum_xy(w_xy, half, rx)
    w_z = []
    for j, (pz, d) in enumerate(z_peers):
        part = pl.ds(pl.multiple_of(pz * tile, tile), tile)
        w_z.append(remote(zbuf.at[:, part], rz_main.at[j + 1], d))

    table_grad(core, sm, dt2, 1)
    d2_core.wait_recv()
    ed2[...] = (dt2[1, 1 - zl].astype(F32) + rd2[1 - zl].astype(F32)).astype(BF)
    d2_z = remote(ed2, re2, zpart)

    zbuf[:, 144:160] = sum_xy(l_xy, half2, rx2)
    l_z = [
        remote(zbuf.at[:, pl.ds(128, 32)], rz_small.at[j + 1], d) for j, (_, d) in enumerate(z_peers)
    ]
    rz_small[0] = zbuf[:, 128:160]

    d_rim.wait_recv()
    own_sum[rim_part] = dt[1, zl, rim_part].astype(F32) + rd[zl, rim_part].astype(F32) + re[rim_part].astype(F32)
    rims_out[...] = own_sum[rim_part].astype(BF)
    to_tails = remote(rims_out.at[low], rims_in.at[0], below)
    to_heads = remote(rims_out.at[high], rims_in.at[1], above)

    for c in w_z:
        c.wait_recv()
    total = zbuf[:, own_rows].astype(F32)
    for j in range(1, Z):
        total = total + rz_main[j].astype(F32)
    full[own_piece, own_rows] = total.astype(BF)
    g_z = [
        remote(full.at[own_piece, own_rows], full.at[own_piece, own_rows], d) for _, d in z_peers
    ]
    for c in l_z:
        c.wait_recv()
    small = rz_small[lax.rem(Z - z, Z)].astype(F32)
    for j in range(1, Z):
        small = small + rz_small[lax.rem(j + Z - z, Z)].astype(F32)
    full[own_piece, 128:160] = small.astype(BF)
    for c in g_z:
        c.wait_recv()
    g_xy = [remote(full.at[own_piece], full.at[own_piece], d) for _, d in xy_peers]

    d2_z.wait_recv()
    sum2 = dt2[1, zl].astype(F32) + rd2[zl].astype(F32) + re2[...].astype(F32)
    rims2_out[...] = sum2[0:OWN].astype(BF)
    to_tails2 = remote(rims2_out.at[low], rims2_in.at[0], below)
    to_heads2 = remote(rims2_out.at[high], rims2_in.at[1], above)
    d_mid.wait_recv()
    own_sum[mid_part] = dt[1, zl, mid_part].astype(F32) + rd[zl, mid_part].astype(F32) + re[mid_part].astype(F32)
    for c in (to_tails, to_heads, to_tails2, to_heads2):
        c.wait_recv()
    narrow = sum2[OWN:] + jnp.concatenate([rims2_in[1].astype(F32), rims2_in[0].astype(F32)], axis=0)
    dproj = own_sum[mid_part] + jnp.concatenate([rims_in[1].astype(F32), rims_in[0].astype(F32)], axis=0)
    dproj = dproj + nn(narrow.astype(BF), wdown2[...])
    coarse = dproj.astype(BF)
    fine = (dproj - coarse.astype(F32)).astype(BF)
    grad_out[...] = (nt(coarse, wa[...]) + nt(fine, wa[...])).astype(BF)

    for c in g_xy:
        c.wait_recv()
    g_core = remote(full.at[mine], full.at[mine], sib)
    g_core.wait_recv()
    full_out[...] = full[...]
    for c in started:
        c.wait_send()


def finish(factor, grad_hbm, full_ref, wdown_ref, gatoms_hbm, gwa_ref, gwd_ref, gwt_ref, gwb_ref, sem):
    through = pltpu.make_async_copy(grad_hbm, gatoms_hbm, sem.at[0])
    through.start()

    def rows_of(first, part):
        return jnp.concatenate(
            [
                jnp.concatenate([full_ref[first + 4 * r + c, part] for c in range(4)], axis=1)
                for r in range(4)
            ],
            axis=0,
        )

    gwt_ref[...] = rows_of(0, slice(128, 144)).astype(F32) * factor
    gwd_ref[...] = rows_of(0, slice(144, 160)).astype(F32) * factor
    gwb_ref[...] = rows_of(16, slice(0, 128)).astype(F32) * factor
    back = tn(rows_of(16, slice(144, 160)), wdown_ref[...])
    gwa_ref[...] = (rows_of(0, slice(0, 128)).astype(F32) + back) * factor
    through.wait()


def per_device(
    slabs, groups,
    atoms, messages, edge_src, edge_dst, trip_in, trip_out, trip_basis, edge_count, trip_count,
    w_a, w_down, w_t, w_b, cotangent,
):
    dims = dims_of(slabs)
    Y, ZH, X = dims
    XY, Z = X * Y, 2 * ZH
    nb, tile = 16 // XY, 128 // Z
    transfers = 32 + 3 * (XY - 1) + 3 * (Z - 1)
    vmem = pl.BlockSpec(memory_space=pltpu.VMEM)
    smem = pl.BlockSpec(memory_space=pltpu.SMEM)
    hbm = pl.BlockSpec(memory_space=pl.ANY)
    index = [a.reshape(16, 128) for a in (edge_src, edge_dst, trip_in, trip_out)]
    w_down = w_down.T
    V = pltpu.VMEM
    full, grad = pl.pallas_call(
        functools.partial(kernel, dims),
        out_shape=(
            jax.ShapeDtypeStruct((32, 160, 128), BF),
            jax.ShapeDtypeStruct((OWN, WIDTH), BF),
        ),
        in_specs=[smem, smem] + [vmem] * 6 + [hbm] * 6,
        out_specs=(vmem, vmem),
        scratch_shapes=[
            V((4, OWN, WIDTH), BF), V((4, OWN, WIDTH), BF), V((4, OWN, WIDTH), BF),
            V((SLOTS, WIDTH), BF), V((DT, SLOTS), BF), V((512, WIDTH), BF), V((512, WIDTH), BF),
            V((SLOTS, WIDTH), BF), V((SLOTS, WIDTH), F32), V((SLOTS, WIDTH), BF),
            V((SLOTS, 128), jnp.int32), V((SLOTS, 128), jnp.int32),
            V((SLOTS, 128), jnp.int32), V((SLOTS, 128), jnp.int32),
            V((8, SLOTS), jnp.int32), V((SLOTS, 128), F32), V((128, WIDTH), BF), V((128, WIDTH), BF),
            V((SLOTS, 128), BF), V((LO, WIDTH), BF), V((LO, WIDTH), F32), V((SLOTS, 128), BF),
            V((2, 2, ROWS, WIDTH), BF), V((2, ROWS, WIDTH), BF), V((ROWS, WIDTH), BF), V((ROWS, WIDTH), BF),
            V((ROWS, WIDTH), F32),
            V((2, 2, ROWS, 128), BF), V((2, ROWS, 128), BF), V((ROWS, 128), BF), V((ROWS, 128), BF),
            V((OWN, WIDTH), BF), V((2, GH, WIDTH), BF), V((OWN, 128), BF), V((2, GH, 128), BF),
            V((512, WIDTH), F32), V((512, WIDTH), F32), V((128, WIDTH), F32), V((128, WIDTH), F32),
            V((128, WIDTH), F32),
            V((32, 144, 128), BF), V((16, 144, 128), BF), V((16, 144, 128), BF),
            V((XY - 1, nb, 144, 128), BF),
            V((32, 16, 128), BF), V((16, 16, 128), BF), V((16, 16, 128), BF), V((XY - 1, nb, 16, 128), BF),
            V((nb, 160, 128), BF), V((Z, nb, tile, 128), BF), V((Z, nb, 32, 128), BF), V((32, 160, 128), BF),
            pltpu.SemaphoreType.DMA((transfers,)), pltpu.SemaphoreType.DMA((transfers,)),
            pltpu.SemaphoreType.DMA((6,)),
        ],
        compiler_params=pltpu.CompilerParams(
            collective_id=0, has_side_effects=True, vmem_limit_bytes=60 * 1024 * 1024
        ),
    )(
        edge_count, trip_count, *index, w_down, w_t,
        atoms, cotangent, messages, trip_basis.T, w_a, w_b,
    )
    factor = 1.0 / math.sqrt(OWN * groups * slabs)
    grad, gwa, gwd, gwt, gwb = pl.pallas_call(
        functools.partial(finish, factor),
        out_shape=(
            jax.ShapeDtypeStruct((OWN, WIDTH), BF),
            jax.ShapeDtypeStruct((512, WIDTH), F32),
            jax.ShapeDtypeStruct((DT, WIDTH), F32),
            jax.ShapeDtypeStruct((DT, WIDTH), F32),
            jax.ShapeDtypeStruct((512, WIDTH), F32),
        ),
        in_specs=[hbm, vmem, vmem],
        out_specs=(hbm, vmem, vmem, vmem, vmem),
        scratch_shapes=[pltpu.SemaphoreType.DMA((1,))],
        compiler_params=pltpu.CompilerParams(vmem_limit_bytes=32 * 1024 * 1024),
    )(grad, full, w_down)
    return grad, gwa, gwd.T, gwt, gwb


def solution(mesh):
    both = P(("dom", "gp"))
    rows = P(("dom", "gp"), None)
    in_specs = (rows, rows, both, both, both, both, rows, both, both, P(), P(), P(), P(), rows)
    out_specs = (rows, P(), P(), P(), P())
    return jax.shard_map(
        functools.partial(per_device, mesh.shape["dom"], mesh.shape["gp"]),
        mesh=mesh, in_specs=in_specs, out_specs=out_specs, check_vma=False,
    )
```

```python
import functools
import math

import jax
import jax.numpy as jnp
from jax import lax
from jax.experimental import pallas as pl
from jax.experimental.pallas import tpu as pltpu
from jax.sharding import PartitionSpec as P

BF = jnp.bfloat16
F32 = jnp.float32
MESH = pl.DeviceIdType.MESH
GH = 128
OWN = 256
ROWS = 512
SLOTS = 2048
WIDTH = 512
DT = 64
LO = 256
BLK = 512


def dims_of(slabs):
    return {64: (4, 4, 4), 4: (1, 1, 4), 2: (1, 1, 2)}[slabs]


def nn(a, b):
    return lax.dot_general(a, b, (((1,), (0,)), ((), ())), preferred_element_type=F32)


def nt(a, b):
    return lax.dot_general(a, b, (((1,), (1,)), ((), ())), preferred_element_type=F32)


def tn(a, b):
    return lax.dot_general(a, b, (((0,), (0,)), ((), ())), preferred_element_type=F32)


def lanes(shape):
    return lax.broadcasted_iota(jnp.int32, shape, len(shape) - 1)


def pick_columns(index, first, width):
    lane = lanes(index.shape)
    local = index - first
    return jnp.concatenate(
        [jnp.where(local == lane + 128 * j, 1.0, 0.0).astype(BF) for j in range(width // 128)], axis=1
    )


def pick_rows(index, first, height):
    shape = (height, index.shape[1])
    row = lax.broadcasted_iota(jnp.int32, shape, 0)
    return jnp.where(row == jnp.broadcast_to(index - first, shape), 1.0, 0.0).astype(BF)


def table_row(src):
    up = src - 1536
    lower = 4 * OWN + ((src >> 7) << 8) + (src & 127)
    upper = 4 * OWN + ((up >> 7) << 8) + GH + (up & 127)
    return jnp.where(src < 512, lower, jnp.where(src < 1536, src - 512, upper))


def kernel(
    dims,
    ecnt_ref, tcnt_ref, src_ref, dst_ref, tin_ref, tout_ref, wdown_ref, wt_ref,
    atoms_hbm, cot_hbm, msg_hbm, basis_hbm, wa_hbm, wb_hbm,
    full_out, grad_out,
    mid, rim, cots, msg, basis, wa, wb, picked, inc, dpre,
    src_col, dst_col, tin_col, tout_col, rows, basis2, wdown2, wt2,
    down, dn, acc_s, sm,
    dt, rd, ed, re, grad, dt2, rd2, ed2, re2, rims_out, rims_in, rims2_out, rims2_in,
    acc_wa, acc_wb, acc_wt, acc_wd, acc_wx, pieces, rc, half, rx, late, rc2, half2, rx2,
    zbuf, rz_main, rz_small, full,
    send, recv, local_sem,
):
    Y, ZH, X = dims
    XY = X * Y
    Z = 2 * ZH
    nb = 16 // XY
    tile = 128 // Z
    dom = lax.axis_index("dom")
    gp = lax.axis_index("gp")
    slabs = Y * ZH * X
    x = lax.rem(dom, X)
    zh = lax.rem(lax.div(dom, X), ZH)
    y = lax.div(dom, X * ZH)
    core = lax.rem(gp, 2)
    zl = lax.div(gp, 2)
    z = zh * 2 + zl

    sib = {"dom": dom, "gp": zl * 2 + (1 - core)}
    zpart = {"dom": dom, "gp": (1 - zl) * 2 + core}
    kz = (1 - zl) * 2 + core
    above = {"dom": lax.rem(dom + 1, slabs), "gp": gp}
    below = {"dom": lax.rem(dom + slabs - 1, slabs), "gp": gp}
    xy_peers = []
    for j in range(1, XY):
        px = lax.rem(x + j // Y, X)
        py = lax.rem(y + j % Y, Y)
        xy_peers.append((px * Y + py, {"dom": (py * ZH + zh) * X + px, "gp": gp}))
    z_peers = []
    for j in range(1, Z):
        pz = lax.rem(z + j, Z)
        z_peers.append((pz, {"dom": (y * ZH + lax.div(pz, 2)) * X + x, "gp": lax.rem(pz, 2) * 2 + core}))

    barrier = pltpu.get_barrier_semaphore()
    others = [sib, above, below] + [d for _, d in xy_peers] + [d for _, d in z_peers]
    for d in others:
        pl.semaphore_signal(barrier, inc=1, device_id=d, device_id_type=MESH)

    count = [0]
    started = []

    def remote(src, dst, device):
        i = count[0]
        count[0] += 1
        c = pltpu.make_async_remote_copy(
            src_ref=src, dst_ref=dst, send_sem=send.at[i], recv_sem=recv.at[i],
            device_id=device, device_id_type=MESH,
        )
        c.start()
        started.append(c)
        return c

    local = []
    for i, (src, dst) in enumerate(
        (
            (atoms_hbm, mid.at[gp]), (cot_hbm, cots.at[gp]), (basis_hbm, basis),
            (wa_hbm, wa), (msg_hbm, msg), (wb_hbm, wb),
        )
    ):
        c = pltpu.make_async_copy(src, dst, local_sem.at[i])
        c.start()
        local.append(c)
    atoms_in, cot_in, basis_in, wa_in, msg_in, wb_in = local

    pl.semaphore_wait(barrier, len(others))

    low = pl.ds(0, GH)
    high = pl.ds(GH, GH)
    to_above = remote(atoms_hbm.at[high], rim.at[gp, low], above)
    to_below = remote(atoms_hbm.at[low], rim.at[gp, high], below)
    to_z = remote(atoms_hbm, mid.at[gp], zpart)
    to_sib = remote(atoms_hbm, mid.at[gp], sib)

    edges = ecnt_ref[...]
    trips = tcnt_ref[...]
    for n, (ref, col) in enumerate(
        ((src_ref, src_col), (dst_ref, dst_col), (tin_ref, tin_col), (tout_ref, tout_col))
    ):
        flat = ref[...]
        if n == 0:
            flat = table_row(flat)
        for j in range(SLOTS // 128):
            line = flat[j : j + 1]
            rows[n : n + 1, 128 * j : 128 * (j + 1)] = line
            col[128 * j : 128 * (j + 1)] = jnp.transpose(jnp.broadcast_to(line, (128, 128)))
    wdown2[...] = jnp.concatenate([wdown_ref[...], wdown_ref[...]], axis=0)
    wt2[...] = jnp.concatenate([wt_ref[...], wt_ref[...]], axis=0)
    basis_in.wait()
    twice = jnp.where(
        lax.broadcasted_iota(jnp.int32, (DT, 128), 0) == (lanes((DT, 128)) & (DT - 1)), 1.0, 0.0
    ).astype(BF)
    valid = lax.broadcasted_iota(jnp.int32, (SLOTS, 128), 0) < jnp.broadcast_to(trips, (SLOTS, 128))
    basis2[...] = jnp.where(valid, tn(basis[...], twice), 0.0)

    atoms_in.wait()
    to_sib.wait_recv()
    to_above.wait_recv()
    z_low = remote(rim.at[gp, low], rim.at[gp, low], zpart)
    s_low = remote(rim.at[gp, low], rim.at[gp, low], sib)
    to_below.wait_recv()
    z_high = remote(rim.at[gp, high], rim.at[gp, high], zpart)
    s_high = remote(rim.at[gp, high], rim.at[gp, high], sib)
    z_cot = remote(cot_hbm, cots.at[gp], zpart)
    s_cot = remote(cot_hbm, cots.at[gp], sib)
    to_z.wait_recv()
    f_mid = remote(mid.at[kz], mid.at[kz], sib)
    f_mid.wait_recv()

    def block(b):
        return pl.ds(pl.multiple_of(b * BLK, BLK), BLK)

    def gather(index, first, source):
        got = nn(pick_columns(index, first, OWN), source[0])
        for k in range(1, 4):
            got = got + nn(pick_columns(index, first + k * OWN, OWN), source[k])
        return got

    def edge_own(b, carry):
        picked[block(b)] = gather(src_col[block(b)], 0, mid).astype(BF)
        return carry

    lax.fori_loop(0, SLOTS // BLK, edge_own, 0)

    z_low.wait_recv()
    f_low = remote(rim.at[kz, low], rim.at[kz, low], sib)
    z_high.wait_recv()
    f_high = remote(rim.at[kz, high], rim.at[kz, high], sib)
    for c in (s_low, s_high, f_low, f_high):
        c.wait_recv()
    wa_in.wait()
    msg_in.wait()

    def row_mask(b, width):
        shape = (BLK, width)
        return lax.broadcasted_iota(jnp.int32, shape, 0) < jnp.broadcast_to(edges - b * BLK, shape)

    def edge_in(b, carry):
        at = block(b)
        got = (picked[at].astype(F32) + gather(src_col[at], 4 * OWN, rim)).astype(BF)
        picked[at] = got
        proj = nn(got, wa[...]).astype(BF).astype(F32)
        value = jnp.where(row_mask(b, WIDTH), proj + msg[at].astype(F32), 0.0)
        inc[at] = value
        down[at] = nt(value.astype(BF), wdown2[...]).astype(BF)
        return carry

    lax.fori_loop(0, SLOTS // BLK, edge_in, 0)
    z_cot.wait_recv()
    f_cot = remote(cots.at[kz], cots.at[kz], sib)

    def pack(source):
        first = lanes((LO, 128)) < DT
        for j in range(4):
            a = source[2 * j * LO : (2 * j + 1) * LO].astype(F32)
            b = source[(2 * j + 1) * LO : (2 * j + 2) * LO].astype(F32)
            dn[:, 128 * j : 128 * (j + 1)] = jnp.where(first, a, b).astype(BF)

    def unpack():
        first = lanes((LO, 128)) < DT
        for j in range(4):
            v = acc_s[:, 128 * j : 128 * (j + 1)]
            sm[2 * j * LO : (2 * j + 1) * LO] = jnp.where(first, v, 0.0).astype(BF)
            sm[(2 * j + 1) * LO : (2 * j + 2) * LO] = jnp.where(first, 0.0, v).astype(BF)

    def triplets(from_col, to_col, to_row):
        half_lane = jnp.where(lanes((BLK, 128)) < DT, 0, 1)
        acc_s[...] = jnp.zeros_like(acc_s)

        def body(b, carry):
            at = block(b)
            frm = from_col[at]
            to = to_col[at]
            got = nn(pick_columns(frm & (LO - 1), 0, LO), dn[...])
            frm_hi = frm >> 8
            to_hi = to >> 8
            value = jnp.where(frm_hi == half_lane, got[:, 0:128], 0.0)
            for j in range(1, 4):
                value = value + jnp.where(
                    frm_hi == half_lane + 2 * j, got[:, 128 * j : 128 * (j + 1)], 0.0
                )
            value = value + pltpu.roll(value, DT, 1)
            value = value * basis2[at]
            spread = jnp.concatenate(
                [jnp.where(to_hi == half_lane + 2 * j, value, 0.0).astype(BF) for j in range(4)], axis=1
            )
            line = rows[to_row : to_row + 1, block(b)]
            acc_s[...] += nn(pick_rows(line & (LO - 1), 0, LO), spread)
            return carry

        lax.fori_loop(0, SLOTS // BLK, body, 0)

    pack(down)
    triplets(tin_col, tout_col, 3)
    unpack()
    cot_in.wait()
    wb_in.wait()
    s_cot.wait_recv()
    f_cot.wait_recv()

    for acc in (acc_wa, acc_wb, acc_wt, acc_wd, acc_wx):
        acc[...] = jnp.zeros_like(acc)

    def edge_mid(b, carry):
        at = block(b)
        mask = row_mask(b, WIDTH)
        cot = gather(dst_col[at], 0, cots).astype(BF)
        atom_grad = nt(cot, wb[...])
        summed = sm[at]
        pre = inc[at] + nn(summed, wt2[...])
        sig = jax.nn.sigmoid(pre)
        out = jnp.where(mask, pre * sig, 0.0).astype(BF)
        grad = jnp.where(mask, atom_grad * sig * (1.0 + pre * (1.0 - sig)), 0.0).astype(BF)
        dpre[at] = grad
        acc_wb[...] += tn(out, cot)
        acc_wa[...] += tn(picked[at], grad)
        acc_wt[...] += tn(summed, grad)
        down[at] = nt(grad, wt2[...]).astype(BF)
        return carry

    lax.fori_loop(0, SLOTS // BLK, edge_mid, 0)

    def fold(acc, r, cols):
        return (acc[16 * r : 16 * (r + 1), cols] + acc[DT + 16 * r : DT + 16 * (r + 1), cols]).astype(BF)

    for s in range(32):
        r, c = (s % 16) // 4, s % 4
        cols = slice(128 * c, 128 * (c + 1))
        pieces[s, 0:128] = (acc_wa if s < 16 else acc_wb)[128 * r : 128 * (r + 1), cols].astype(BF)
        pieces[s, 128:144] = fold(acc_wt, r, cols) if s < 16 else jnp.zeros((16, 128), BF)
    not_mine = pl.ds((1 - core) * 16, 16)
    mine = pl.ds(core * 16, 16)
    w_core = remote(pieces.at[not_mine], rc, sib)

    def table_grad(owner, source, out, who):
        for part in range(2):
            first = (4 + owner) * OWN if part == 0 else owner * OWN
            total = None
            for b in range(SLOTS // BLK):
                cols = slice(BLK * b, BLK * (b + 1))
                line = rows[0:1, cols]
                choice = jnp.concatenate(
                    [pick_rows(line, first, OWN), pick_rows(line, first + 2 * OWN, OWN)], axis=0
                )
                term = nn(choice, source[cols])
                total = term if total is None else total + term
            total = total.astype(BF)
            out[who, 0, OWN * part : OWN * (part + 1)] = total[0:OWN]
            out[who, 1, OWN * part : OWN * (part + 1)] = total[OWN:]

    table_grad(1 - core, dpre, dt, 0)
    d_core = remote(dt.at[0], rd, sib)
    w_core.wait_recv()
    half[...] = (pieces[mine].astype(F32) + rc[...].astype(F32)).astype(BF)
    w_xy = [
        remote(half.at[pl.ds(s * nb, nb)], rx.at[j], d) for j, (s, d) in enumerate(xy_peers)
    ]
    table_grad(core, dpre, dt, 1)
    d_core.wait_recv()
    ed[...] = (dt[1, 1 - zl].astype(F32) + rd[1 - zl].astype(F32)).astype(BF)
    rim_part = pl.ds(0, OWN)
    mid_part = pl.ds(OWN, OWN)
    d_rim = remote(ed.at[rim_part], re.at[rim_part], zpart)

    pack(down)
    triplets(tout_col, tin_col, 2)
    unpack()

    def edge_out(b, carry):
        at = block(b)
        back = jnp.where(row_mask(b, 128), sm[at].astype(F32), 0.0).astype(BF)
        sm[at] = back
        acc_wd[...] += tn(back, inc[at].astype(BF))
        acc_wx[...] += tn(back, picked[at])
        return carry

    lax.fori_loop(0, SLOTS // BLK, edge_out, 0)
    for s in range(32):
        r, c = (s % 16) // 4, s % 4
        late[s] = fold(acc_wd if s < 16 else acc_wx, r, slice(128 * c, 128 * (c + 1)))
    l_core = remote(late.at[not_mine], rc2, sib)
    table_grad(1 - core, sm, dt2, 0)
    d2_core = remote(dt2.at[0], rd2, sib)
    l_core.wait_recv()
    half2[...] = (late[mine].astype(F32) + rc2[...].astype(F32)).astype(BF)
    l_xy = [
        remote(half2.at[pl.ds(s * nb, nb)], rx2.at[j], d) for j, (s, d) in enumerate(xy_peers)
    ]

    own_s = x * Y + y
    own_rows = pl.ds(pl.multiple_of(z * tile, tile), tile)
    own_piece = pl.ds(core * 16 + own_s * nb, nb)

    def sum_xy(copies, buffer, received):
        for c in copies:
            c.wait_recv()
        total = buffer[pl.ds(own_s * nb, nb)].astype(F32)
        for j in range(XY - 1):
            total = total + received[j].astype(F32)
        return total.astype(BF)

    zbuf[:, 0:144] = sum_xy(w_xy, half, rx)
    w_z = []
    for j, (pz, d) in enumerate(z_peers):
        part = pl.ds(pl.multiple_of(pz * tile, tile), tile)
        w_z.append(remote(zbuf.at[:, part], rz_main.at[j + 1], d))
    d_mid = remote(ed.at[mid_part], re.at[mid_part], zpart)

    table_grad(core, sm, dt2, 1)
    zbuf[:, 144:160] = sum_xy(l_xy, half2, rx2)
    l_z = [
        remote(zbuf.at[:, pl.ds(128, 32)], rz_small.at[j + 1], d) for j, (_, d) in enumerate(z_peers)
    ]
    rz_small[0] = zbuf[:, 128:160]
    d2_core.wait_recv()
    ed2[...] = (dt2[1, 1 - zl].astype(F32) + rd2[1 - zl].astype(F32)).astype(BF)
    d2_z = remote(ed2, re2, zpart)

    for c in w_z:
        c.wait_recv()
    total = zbuf[:, own_rows].astype(F32)
    for j in range(1, Z):
        total = total + rz_main[j].astype(F32)
    full[own_piece, own_rows] = total.astype(BF)
    g_z = [
        remote(full.at[own_piece, own_rows], full.at[own_piece, own_rows], d) for _, d in z_peers
    ]

    d_rim.wait_recv()
    rims_out[...] = (
        dt[1, zl, rim_part].astype(F32) + rd[zl, rim_part].astype(F32) + re[rim_part].astype(F32)
    ).astype(BF)
    to_tails = remote(rims_out.at[low], rims_in.at[0], below)
    to_heads = remote(rims_out.at[high], rims_in.at[1], above)

    for c in l_z:
        c.wait_recv()
    small = rz_small[lax.rem(Z - z, Z)].astype(F32)
    for j in range(1, Z):
        small = small + rz_small[lax.rem(j + Z - z, Z)].astype(F32)
    full[own_piece, 128:160] = small.astype(BF)
    for c in g_z:
        c.wait_recv()
    g_xy = [remote(full.at[own_piece], full.at[own_piece], d) for _, d in xy_peers]
    g_core = [remote(full.at[own_piece], full.at[own_piece], sib)]

    d2_z.wait_recv()
    sum2 = dt2[1, zl].astype(F32) + rd2[zl].astype(F32) + re2[...].astype(F32)
    rims2_out[...] = sum2[0:OWN].astype(BF)
    to_tails2 = remote(rims2_out.at[low], rims2_in.at[0], below)
    to_heads2 = remote(rims2_out.at[high], rims2_in.at[1], above)

    for j, c in enumerate(g_xy):
        c.wait_recv()
        px = lax.rem(x + X - (j + 1) // Y, X)
        py = lax.rem(y + Y - (j + 1) % Y, Y)
        piece = pl.ds(core * 16 + (px * Y + py) * nb, nb)
        g_core.append(remote(full.at[piece], full.at[piece], sib))

    d_mid.wait_recv()
    for c in (to_tails, to_heads, to_tails2, to_heads2):
        c.wait_recv()
    narrow = sum2[OWN:] + jnp.concatenate([rims2_in[1].astype(F32), rims2_in[0].astype(F32)], axis=0)
    dproj = dt[1, zl, mid_part].astype(F32) + rd[zl, mid_part].astype(F32) + re[mid_part].astype(F32)
    dproj = dproj + jnp.concatenate([rims_in[1].astype(F32), rims_in[0].astype(F32)], axis=0)
    dproj = dproj + nn(narrow.astype(BF), wdown2[...])
    coarse = dproj.astype(BF)
    fine = (dproj - coarse.astype(F32)).astype(BF)
    grad[...] = (nt(coarse, wa[...]) + nt(fine, wa[...])).astype(BF)
    grad_copy = pltpu.make_async_copy(grad, grad_out, local_sem.at[6])
    grad_copy.start()

    for c in g_core:
        c.wait_recv()
    full_copy = pltpu.make_async_copy(full, full_out, local_sem.at[7])
    full_copy.start()
    for c in started:
        c.wait_send()
    grad_copy.wait()
    full_copy.wait()


def finish(
    factor, grad_hbm, full_hbm, wdown_ref, gatoms_hbm, gwa_hbm, gwd_hbm, gwt_hbm, gwb_hbm,
    full, gwa, gwd, gwt, gwb, sem,
):
    copies = []

    def copy(src, dst):
        c = pltpu.make_async_copy(src, dst, sem.at[len(copies)])
        c.start()
        copies.append(c)
        return c

    second = copy(full_hbm.at[pl.ds(16, 16)], full.at[pl.ds(16, 16)])
    first = copy(full_hbm.at[pl.ds(0, 16)], full.at[pl.ds(0, 16)])
    copy(grad_hbm, gatoms_hbm)

    def rows_of(first, part):
        return jnp.concatenate(
            [
                jnp.concatenate([full[first + 4 * r + c, part] for c in range(4)], axis=1)
                for r in range(4)
            ],
            axis=0,
        )

    second.wait()
    gwb[...] = rows_of(16, slice(0, 128)).astype(F32) * factor
    copy(gwb, gwb_hbm)
    back = tn(rows_of(16, slice(144, 160)), wdown_ref[...])
    first.wait()
    gwa[...] = (rows_of(0, slice(0, 128)).astype(F32) + back) * factor
    copy(gwa, gwa_hbm)
    gwt[...] = rows_of(0, slice(128, 144)).astype(F32) * factor
    copy(gwt, gwt_hbm)
    gwd[...] = rows_of(0, slice(144, 160)).astype(F32) * factor
    copy(gwd, gwd_hbm)
    for c in copies[2:]:
        c.wait()


def per_device(
    slabs, groups,
    atoms, messages, edge_src, edge_dst, trip_in, trip_out, trip_basis, edge_count, trip_count,
    w_a, w_down, w_t, w_b, cotangent,
):
    dims = dims_of(slabs)
    Y, ZH, X = dims
    XY, Z = X * Y, 2 * ZH
    nb, tile = 16 // XY, 128 // Z
    transfers = 32 + 4 * (XY - 1) + 3 * (Z - 1)
    vmem = pl.BlockSpec(memory_space=pltpu.VMEM)
    hbm = pl.BlockSpec(memory_space=pl.ANY)
    index = [a.reshape(16, 128) for a in (edge_src, edge_dst, trip_in, trip_out)]
    w_down = w_down.T
    V = pltpu.VMEM
    full, grad = pl.pallas_call(
        functools.partial(kernel, dims),
        out_shape=(
            jax.ShapeDtypeStruct((32, 160, 128), BF),
            jax.ShapeDtypeStruct((OWN, WIDTH), BF),
        ),
        in_specs=[vmem] * 8 + [hbm] * 6,
        out_specs=(hbm, hbm),
        scratch_shapes=[
            V((4, OWN, WIDTH), BF), V((4, OWN, WIDTH), BF), V((4, OWN, WIDTH), BF),
            V((SLOTS, WIDTH), BF), V((DT, SLOTS), BF), V((512, WIDTH), BF), V((512, WIDTH), BF),
            V((SLOTS, WIDTH), BF), V((SLOTS, WIDTH), F32), V((SLOTS, WIDTH), BF),
            V((SLOTS, 128), jnp.int32), V((SLOTS, 128), jnp.int32),
            V((SLOTS, 128), jnp.int32), V((SLOTS, 128), jnp.int32),
            V((8, SLOTS), jnp.int32), V((SLOTS, 128), F32), V((128, WIDTH), BF), V((128, WIDTH), BF),
            V((SLOTS, 128), BF), V((LO, WIDTH), BF), V((LO, WIDTH), F32), V((SLOTS, 128), BF),
            V((2, 2, ROWS, WIDTH), BF), V((2, ROWS, WIDTH), BF), V((ROWS, WIDTH), BF), V((ROWS, WIDTH), BF),
            V((OWN, WIDTH), BF),
            V((2, 2, ROWS, 128), BF), V((2, ROWS, 128), BF), V((ROWS, 128), BF), V((ROWS, 128), BF),
            V((OWN, WIDTH), BF), V((2, GH, WIDTH), BF), V((OWN, 128), BF), V((2, GH, 128), BF),
            V((512, WIDTH), F32), V((512, WIDTH), F32), V((128, WIDTH), F32), V((128, WIDTH), F32),
            V((128, WIDTH), F32),
            V((32, 144, 128), BF), V((16, 144, 128), BF), V((16, 144, 128), BF),
            V((XY - 1, nb, 144, 128), BF),
            V((32, 16, 128), BF), V((16, 16, 128), BF), V((16, 16, 128), BF), V((XY - 1, nb, 16, 128), BF),
            V((nb, 160, 128), BF), V((Z, nb, tile, 128), BF), V((Z, nb, 32, 128), BF), V((32, 160, 128), BF),
            pltpu.SemaphoreType.DMA((transfers,)), pltpu.SemaphoreType.DMA((transfers,)),
            pltpu.SemaphoreType.DMA((8,)),
        ],
        compiler_params=pltpu.CompilerParams(
            collective_id=0, has_side_effects=True, vmem_limit_bytes=60 * 1024 * 1024
        ),
    )(
        edge_count.reshape(1, 1), trip_count.reshape(1, 1), *index, w_down, w_t,
        atoms, cotangent, messages, trip_basis.T, w_a, w_b,
    )
    factor = 1.0 / math.sqrt(OWN * groups * slabs)
    grad, gwa, gwd, gwt, gwb = pl.pallas_call(
        functools.partial(finish, factor),
        out_shape=(
            jax.ShapeDtypeStruct((OWN, WIDTH), BF),
            jax.ShapeDtypeStruct((512, WIDTH), F32),
            jax.ShapeDtypeStruct((DT, WIDTH), F32),
            jax.ShapeDtypeStruct((DT, WIDTH), F32),
            jax.ShapeDtypeStruct((512, WIDTH), F32),
        ),
        in_specs=[hbm, hbm, vmem],
        out_specs=(hbm,) * 5,
        scratch_shapes=[
            V((32, 160, 128), BF), V((512, WIDTH), F32), V((DT, WIDTH), F32), V((DT, WIDTH), F32),
            V((512, WIDTH), F32), pltpu.SemaphoreType.DMA((8,)),
        ],
        compiler_params=pltpu.CompilerParams(vmem_limit_bytes=60 * 1024 * 1024),
    )(grad, full, w_down)
    return grad, gwa, gwd.T, gwt, gwb


def solution(mesh):
    both = P(("dom", "gp"))
    rows = P(("dom", "gp"), None)
    in_specs = (rows, rows, both, both, both, both, rows, both, both, P(), P(), P(), P(), rows)
    out_specs = (rows, P(), P(), P(), P())
    return jax.shard_map(
        functools.partial(per_device, mesh.shape["dom"], mesh.shape["gp"]),
        mesh=mesh, in_specs=in_specs, out_specs=out_specs, check_vma=False,
    )
```

```python
import functools
import math

import jax
import jax.numpy as jnp
from jax import lax
from jax.experimental import pallas as pl
from jax.experimental.pallas import tpu as pltpu
from jax.sharding import PartitionSpec as P

BF = jnp.bfloat16
F32 = jnp.float32
MESH = pl.DeviceIdType.MESH
GH = 128
OWN = 256
ROWS = 512
SLOTS = 2048
WIDTH = 512
DT = 64
LO = 256
BLK = 512


def dims_of(slabs):
    return {64: (4, 4, 4), 4: (1, 1, 4), 2: (1, 1, 2)}[slabs]


def nn(a, b):
    return lax.dot_general(a, b, (((1,), (0,)), ((), ())), preferred_element_type=F32)


def nt(a, b):
    return lax.dot_general(a, b, (((1,), (1,)), ((), ())), preferred_element_type=F32)


def tn(a, b):
    return lax.dot_general(a, b, (((0,), (0,)), ((), ())), preferred_element_type=F32)


def lanes(shape):
    return lax.broadcasted_iota(jnp.int32, shape, len(shape) - 1)


def pick_columns(index, first, width):
    lane = lanes(index.shape)
    local = index - first
    return jnp.concatenate(
        [jnp.where(local == lane + 128 * j, 1.0, 0.0).astype(BF) for j in range(width // 128)], axis=1
    )


def pick_rows(index, first, height):
    shape = (height, index.shape[1])
    row = lax.broadcasted_iota(jnp.int32, shape, 0)
    return jnp.where(row == jnp.broadcast_to(index - first, shape), 1.0, 0.0).astype(BF)


def table_row(src):
    up = src - 1536
    lower = 4 * OWN + ((src >> 7) << 8) + (src & 127)
    upper = 4 * OWN + ((up >> 7) << 8) + GH + (up & 127)
    return jnp.where(src < 512, lower, jnp.where(src < 1536, src - 512, upper))


def kernel(
    dims,
    ecnt_ref, tcnt_ref, src_ref, dst_ref, tin_ref, tout_ref, wdown_ref, wt_ref,
    atoms_hbm, cot_hbm, msg_hbm, basis_hbm, wa_hbm, wb_hbm,
    full_a_out, full_b_out, grad_out,
    mid, rim, cots, msg, basis, wa, wb, picked, inc, dpre,
    src_col, dst_col, tin_col, tout_col, rows, basis2, wdown2, wt2,
    down, dn, acc_s, sm,
    dt, rd, ed, re, grad, dt2, rd2, ed2, re2, rims_out, rims_in, rims2_out, rims2_in,
    acc_wa, acc_wb, acc_wt, acc_wd, acc_wx, picked_cot, slope,
    pieces_b, rc_b, half_b, rx_b, z_b, rz_b, fz_b, full_b,
    pieces_a, rc_a, half_a, rx_a, z_a, rz_a, fz_a, full_a,
    late, rc_l, half_l, rx_l, small_z, rz_small,
    send, recv, local_sem,
):
    Y, ZH, X = dims
    XY = X * Y
    Z = 2 * ZH
    nb = 16 // XY
    tile = 64 // Z
    dom = lax.axis_index("dom")
    gp = lax.axis_index("gp")
    slabs = Y * ZH * X
    x = lax.rem(dom, X)
    zh = lax.rem(lax.div(dom, X), ZH)
    y = lax.div(dom, X * ZH)
    core = lax.rem(gp, 2)
    zl = lax.div(gp, 2)
    z = zh * 2 + zl

    sib = {"dom": dom, "gp": zl * 2 + (1 - core)}
    zpart = {"dom": dom, "gp": (1 - zl) * 2 + core}
    kz = (1 - zl) * 2 + core
    above = {"dom": lax.rem(dom + 1, slabs), "gp": gp}
    below = {"dom": lax.rem(dom + slabs - 1, slabs), "gp": gp}
    xy_peers = []
    for j in range(1, XY):
        px = lax.rem(x + j // Y, X)
        py = lax.rem(y + j % Y, Y)
        xy_peers.append((px * Y + py, {"dom": (py * ZH + zh) * X + px, "gp": gp}))
    z_peers = []
    for j in range(1, Z):
        pz = lax.rem(z + j, Z)
        z_peers.append((pz, {"dom": (y * ZH + lax.div(pz, 2)) * X + x, "gp": lax.rem(pz, 2) * 2 + core}))

    barrier = pltpu.get_barrier_semaphore()
    others = [sib, above, below] + [d for _, d in xy_peers] + [d for _, d in z_peers]
    for d in others:
        pl.semaphore_signal(barrier, inc=1, device_id=d, device_id_type=MESH)

    count = [0]
    started = []

    def remote(src, dst, device):
        i = count[0]
        count[0] += 1
        c = pltpu.make_async_remote_copy(
            src_ref=src, dst_ref=dst, send_sem=send.at[i], recv_sem=recv.at[i],
            device_id=device, device_id_type=MESH,
        )
        c.start()
        started.append(c)
        return c

    local = []
    for i, (src, dst) in enumerate(
        (
            (atoms_hbm, mid.at[gp]), (cot_hbm, cots.at[gp]), (basis_hbm, basis),
            (wa_hbm, wa), (msg_hbm, msg), (wb_hbm, wb),
        )
    ):
        c = pltpu.make_async_copy(src, dst, local_sem.at[i])
        c.start()
        local.append(c)
    atoms_in, cot_in, basis_in, wa_in, msg_in, wb_in = local

    pl.semaphore_wait(barrier, len(others))

    low = pl.ds(0, GH)
    high = pl.ds(GH, GH)
    to_above = remote(atoms_hbm.at[high], rim.at[gp, low], above)
    to_below = remote(atoms_hbm.at[low], rim.at[gp, high], below)
    to_z = remote(atoms_hbm, mid.at[gp], zpart)
    to_sib = remote(atoms_hbm, mid.at[gp], sib)

    edges = ecnt_ref[...]
    trips = tcnt_ref[...]
    for n, (ref, col) in enumerate(
        ((src_ref, src_col), (dst_ref, dst_col), (tin_ref, tin_col), (tout_ref, tout_col))
    ):
        flat = ref[...]
        if n == 0:
            flat = table_row(flat)
        for j in range(SLOTS // 128):
            line = flat[j : j + 1]
            rows[n : n + 1, 128 * j : 128 * (j + 1)] = line
            col[128 * j : 128 * (j + 1)] = jnp.transpose(jnp.broadcast_to(line, (128, 128)))
    wdown2[...] = jnp.concatenate([wdown_ref[...], wdown_ref[...]], axis=0)
    wt2[...] = jnp.concatenate([wt_ref[...], wt_ref[...]], axis=0)
    basis_in.wait()
    twice = jnp.where(
        lax.broadcasted_iota(jnp.int32, (DT, 128), 0) == (lanes((DT, 128)) & (DT - 1)), 1.0, 0.0
    ).astype(BF)
    valid = lax.broadcasted_iota(jnp.int32, (SLOTS, 128), 0) < jnp.broadcast_to(trips, (SLOTS, 128))
    basis2[...] = jnp.where(valid, tn(basis[...], twice), 0.0)

    atoms_in.wait()
    to_sib.wait_recv()
    to_above.wait_recv()
    z_low = remote(rim.at[gp, low], rim.at[gp, low], zpart)
    s_low = remote(rim.at[gp, low], rim.at[gp, low], sib)
    to_below.wait_recv()
    z_high = remote(rim.at[gp, high], rim.at[gp, high], zpart)
    s_high = remote(rim.at[gp, high], rim.at[gp, high], sib)
    z_cot = remote(cot_hbm, cots.at[gp], zpart)
    s_cot = remote(cot_hbm, cots.at[gp], sib)
    to_z.wait_recv()
    f_mid = remote(mid.at[kz], mid.at[kz], sib)
    f_mid.wait_recv()

    def block(b):
        return pl.ds(pl.multiple_of(b * BLK, BLK), BLK)

    def gather(index, first, source):
        got = nn(pick_columns(index, first, OWN), source[0])
        for k in range(1, 4):
            got = got + nn(pick_columns(index, first + k * OWN, OWN), source[k])
        return got

    def edge_own(b, carry):
        picked[block(b)] = gather(src_col[block(b)], 0, mid).astype(BF)
        return carry

    lax.fori_loop(0, SLOTS // BLK, edge_own, 0)

    z_low.wait_recv()
    f_low = remote(rim.at[kz, low], rim.at[kz, low], sib)
    z_high.wait_recv()
    f_high = remote(rim.at[kz, high], rim.at[kz, high], sib)
    for c in (s_low, s_high, f_low, f_high):
        c.wait_recv()
    wa_in.wait()
    msg_in.wait()

    def row_mask(b, width):
        shape = (BLK, width)
        return lax.broadcasted_iota(jnp.int32, shape, 0) < jnp.broadcast_to(edges - b * BLK, shape)

    def edge_in(b, carry):
        at = block(b)
        got = (picked[at].astype(F32) + gather(src_col[at], 4 * OWN, rim)).astype(BF)
        picked[at] = got
        proj = nn(got, wa[...]).astype(BF).astype(F32)
        value = jnp.where(row_mask(b, WIDTH), proj + msg[at].astype(F32), 0.0)
        inc[at] = value
        down[at] = nt(value.astype(BF), wdown2[...]).astype(BF)
        return carry

    lax.fori_loop(0, SLOTS // BLK, edge_in, 0)
    z_cot.wait_recv()
    f_cot = remote(cots.at[kz], cots.at[kz], sib)

    def pack(source):
        first = lanes((LO, 128)) < DT
        for j in range(4):
            a = source[2 * j * LO : (2 * j + 1) * LO].astype(F32)
            b = source[(2 * j + 1) * LO : (2 * j + 2) * LO].astype(F32)
            dn[:, 128 * j : 128 * (j + 1)] = jnp.where(first, a, b).astype(BF)

    def unpack():
        first = lanes((LO, 128)) < DT
        for j in range(4):
            v = acc_s[:, 128 * j : 128 * (j + 1)]
            sm[2 * j * LO : (2 * j + 1) * LO] = jnp.where(first, v, 0.0).astype(BF)
            sm[(2 * j + 1) * LO : (2 * j + 2) * LO] = jnp.where(first, 0.0, v).astype(BF)

    def triplets(from_col, to_col, to_row):
        half_lane = jnp.where(lanes((BLK, 128)) < DT, 0, 1)
        acc_s[...] = jnp.zeros_like(acc_s)

        def body(b, carry):
            at = block(b)
            frm = from_col[at]
            to = to_col[at]
            got = nn(pick_columns(frm & (LO - 1), 0, LO), dn[...])
            frm_hi = frm >> 8
            to_hi = to >> 8
            value = jnp.where(frm_hi == half_lane, got[:, 0:128], 0.0)
            for j in range(1, 4):
                value = value + jnp.where(
                    frm_hi == half_lane + 2 * j, got[:, 128 * j : 128 * (j + 1)], 0.0
                )
            value = value + pltpu.roll(value, DT, 1)
            value = value * basis2[at]
            spread = jnp.concatenate(
                [jnp.where(to_hi == half_lane + 2 * j, value, 0.0).astype(BF) for j in range(4)], axis=1
            )
            line = rows[to_row : to_row + 1, block(b)]
            acc_s[...] += nn(pick_rows(line & (LO - 1), 0, LO), spread)
            return carry

        lax.fori_loop(0, SLOTS // BLK, body, 0)

    pack(down)
    triplets(tin_col, tout_col, 3)
    unpack()
    cot_in.wait()
    wb_in.wait()
    s_cot.wait_recv()
    f_cot.wait_recv()

    for acc in (acc_wa, acc_wb, acc_wt, acc_wd, acc_wx):
        acc[...] = jnp.zeros_like(acc)

    not_mine = pl.ds((1 - core) * 16, 16)
    mine = pl.ds(core * 16, 16)
    own_s = x * Y + y
    own_nb = pl.ds(own_s * nb, nb)
    own_piece = pl.ds(core * 16 + own_s * nb, nb)
    own_rows = pl.ds(pl.multiple_of(z * tile, tile), tile)

    def reduce_core(copy, pieces, received, half, got):
        copy.wait_recv()
        half[...] = (pieces[mine].astype(F32) + received[...].astype(F32)).astype(BF)
        return [
            remote(half.at[pl.ds(s * nb, nb)], got.at[j], d) for j, (s, d) in enumerate(xy_peers)
        ]

    def sum_xy(copies, half, got):
        for c in copies:
            c.wait_recv()
        total = half[own_nb].astype(F32)
        for j in range(XY - 1):
            total = total + got[j].astype(F32)
        return total

    def send_z(buffer, got):
        return [
            remote(buffer.at[:, pl.ds(pl.multiple_of(pz * tile, tile), tile)], got.at[j], d)
            for j, (pz, d) in enumerate(z_peers)
        ]

    def sum_z(copies, buffer, got, whole):
        for c in copies:
            c.wait_recv()
        total = buffer[:, own_rows]
        for j in range(Z - 1):
            total = total + got[j]
        whole[:, own_rows] = total
        return [remote(whole.at[:, own_rows], whole.at[:, own_rows], d) for _, d in z_peers]

    def spread(full):
        own = full.at[own_piece]
        return [remote(own, own, d) for _, d in xy_peers], [remote(own, own, sib)]

    def forward(copies, to_core, full):
        for j, c in enumerate(copies):
            c.wait_recv()
            px = lax.rem(x + X - (j + 1) // Y, X)
            py = lax.rem(y + Y - (j + 1) % Y, Y)
            piece = full.at[pl.ds(core * 16 + (px * Y + py) * nb, nb)]
            to_core.append(remote(piece, piece, sib))

    def fold(acc, r, cols):
        return (acc[16 * r : 16 * (r + 1), cols] + acc[DT + 16 * r : DT + 16 * (r + 1), cols]).astype(BF)

    def edge_mid(b, carry):
        at = block(b)
        mask = row_mask(b, WIDTH)
        cot = gather(dst_col[at], 0, cots).astype(BF)
        picked_cot[at] = cot
        pre = inc[at] + nn(sm[at], wt2[...])
        sig = jax.nn.sigmoid(pre)
        out = jnp.where(mask, pre * sig, 0.0).astype(BF)
        slope[at] = jnp.where(mask, sig * (1.0 + pre * (1.0 - sig)), 0.0)
        acc_wb[...] += tn(out, cot)
        return carry

    lax.fori_loop(0, SLOTS // BLK, edge_mid, 0)
    for s in range(32):
        r, cols = s // 4, slice(128 * (s % 4), 128 * (s % 4 + 1))
        pieces_b[s] = acc_wb[64 * r : 64 * (r + 1), cols].astype(BF)
    b_core = remote(pieces_b.at[not_mine], rc_b, sib)

    def edge_grad(b, carry):
        at = block(b)
        grad = (nt(picked_cot[at], wb[...]) * slope[at]).astype(BF)
        dpre[at] = grad
        acc_wa[...] += tn(picked[at], grad)
        acc_wt[...] += tn(sm[at], grad)
        down[at] = nt(grad, wt2[...]).astype(BF)
        return carry

    lax.fori_loop(0, 2, edge_grad, 0)
    b_xy = reduce_core(b_core, pieces_b, rc_b, half_b, rx_b)
    lax.fori_loop(2, SLOTS // BLK, edge_grad, 0)

    for s in range(32):
        r, cols = s // 4, slice(128 * (s % 4), 128 * (s % 4 + 1))
        pieces_a[s, 0:64] = acc_wa[64 * r : 64 * (r + 1), cols].astype(BF)
        pieces_a[s, 64:80] = fold(acc_wt, r, cols) if s < 16 else jnp.zeros((16, 128), BF)
    a_core = remote(pieces_a.at[not_mine], rc_a, sib)

    def table_grad(owner, source, out, who):
        for part in range(2):
            first = (4 + owner) * OWN if part == 0 else owner * OWN
            total = None
            for b in range(SLOTS // BLK):
                cols = slice(BLK * b, BLK * (b + 1))
                line = rows[0:1, cols]
                choice = jnp.concatenate(
                    [pick_rows(line, first, OWN), pick_rows(line, first + 2 * OWN, OWN)], axis=0
                )
                term = nn(choice, source[cols])
                total = term if total is None else total + term
            total = total.astype(BF)
            out[who, 0, OWN * part : OWN * (part + 1)] = total[0:OWN]
            out[who, 1, OWN * part : OWN * (part + 1)] = total[OWN:]

    table_grad(1 - core, dpre, dt, 0)
    d_core = remote(dt.at[0], rd, sib)
    a_xy = reduce_core(a_core, pieces_a, rc_a, half_a, rx_a)
    z_b[...] = sum_xy(b_xy, half_b, rx_b)
    b_z = send_z(z_b, rz_b)
    table_grad(core, dpre, dt, 1)
    d_core.wait_recv()
    ed[...] = (dt[1, 1 - zl].astype(F32) + rd[1 - zl].astype(F32)).astype(BF)
    rim_part = pl.ds(0, OWN)
    mid_part = pl.ds(OWN, OWN)
    g_bz = sum_z(b_z, z_b, rz_b, fz_b)
    d_rim = remote(ed.at[rim_part], re.at[rim_part], zpart)

    pack(down)
    triplets(tout_col, tin_col, 2)
    unpack()

    for c in g_bz:
        c.wait_recv()
    full_b[own_piece] = fz_b[...].astype(BF)
    g_bxy, g_bcore = spread(full_b)

    def edge_out(b, carry):
        at = block(b)
        back = jnp.where(row_mask(b, 128), sm[at].astype(F32), 0.0).astype(BF)
        sm[at] = back
        acc_wd[...] += tn(back, inc[at].astype(BF))
        acc_wx[...] += tn(back, picked[at])
        return carry

    lax.fori_loop(0, SLOTS // BLK, edge_out, 0)
    for s in range(32):
        r, c = (s % 16) // 4, s % 4
        late[s] = fold(acc_wd if s < 16 else acc_wx, r, slice(128 * c, 128 * (c + 1)))
    l_core = remote(late.at[not_mine], rc_l, sib)

    total_a = sum_xy(a_xy, half_a, rx_a)
    z_a[...] = total_a[:, 0:64]
    small_z[:, 0:16] = total_a[:, 64:80].astype(BF)
    a_z = send_z(z_a, rz_a)
    d_mid = remote(ed.at[mid_part], re.at[mid_part], zpart)

    table_grad(1 - core, sm, dt2, 0)
    d2_core = remote(dt2.at[0], rd2, sib)
    l_xy = reduce_core(l_core, late, rc_l, half_l, rx_l)
    g_az = sum_z(a_z, z_a, rz_a, fz_a)
    table_grad(core, sm, dt2, 1)

    small_z[:, 16:32] = sum_xy(l_xy, half_l, rx_l).astype(BF)
    l_z = [remote(small_z, rz_small.at[j + 1], d) for j, (_, d) in enumerate(z_peers)]
    rz_small[0] = small_z[...]

    def narrow_pack(v):
        v = v + pltpu.roll(v, DT, 1)
        return jnp.where(lanes((OWN, 128)) < DT, v[0:OWN], v[OWN:])

    d2_core.wait_recv()
    ed2[...] = narrow_pack(dt2[1, 1 - zl].astype(F32) + rd2[1 - zl].astype(F32)).astype(BF)
    d2_z = remote(ed2, re2, zpart)

    d_rim.wait_recv()
    rims_out[...] = (
        dt[1, zl, rim_part].astype(F32) + rd[zl, rim_part].astype(F32) + re[rim_part].astype(F32)
    ).astype(BF)
    to_tails = remote(rims_out.at[low], rims_in.at[0], below)
    to_heads = remote(rims_out.at[high], rims_in.at[1], above)

    for c in l_z:
        c.wait_recv()
    small = rz_small[lax.rem(Z - z, Z)].astype(F32)
    for j in range(1, Z):
        small = small + rz_small[lax.rem(j + Z - z, Z)].astype(F32)
    for c in g_az:
        c.wait_recv()
    full_a[own_piece, 0:64] = fz_a[...].astype(BF)
    full_a[own_piece, 64:96] = small.astype(BF)
    g_axy, g_acore = spread(full_a)
    forward(g_bxy, g_bcore, full_b)

    d2_z.wait_recv()
    sum2 = narrow_pack(dt2[1, zl].astype(F32) + rd2[zl].astype(F32)) + re2[...].astype(F32)
    is_rim = lanes((OWN, 128)) < DT
    rims2_out[...] = jnp.where(is_rim, sum2, 0.0).astype(BF)
    to_tails2 = remote(rims2_out.at[low], rims2_in.at[0], below)
    to_heads2 = remote(rims2_out.at[high], rims2_in.at[1], above)
    for c in g_bcore:
        c.wait_recv()
    b_copy = pltpu.make_async_copy(full_b, full_b_out, local_sem.at[8])
    b_copy.start()
    forward(g_axy, g_acore, full_a)

    d_mid.wait_recv()
    for c in (to_tails, to_heads, to_tails2, to_heads2):
        c.wait_recv()
    rims2 = jnp.concatenate([rims2_in[1].astype(F32), rims2_in[0].astype(F32)], axis=0)
    narrow = jnp.where(is_rim, 0.0, sum2) + rims2
    dproj = dt[1, zl, mid_part].astype(F32) + rd[zl, mid_part].astype(F32) + re[mid_part].astype(F32)
    dproj = dproj + jnp.concatenate([rims_in[1].astype(F32), rims_in[0].astype(F32)], axis=0)
    dproj = dproj + nn(narrow.astype(BF), wdown2[...])
    coarse = dproj.astype(BF)
    fine = (dproj - coarse.astype(F32)).astype(BF)
    grad[...] = (nt(coarse, wa[...]) + nt(fine, wa[...])).astype(BF)
    grad_copy = pltpu.make_async_copy(grad, grad_out, local_sem.at[6])
    grad_copy.start()

    for c in g_acore:
        c.wait_recv()
    a_copy = pltpu.make_async_copy(full_a, full_a_out, local_sem.at[7])
    a_copy.start()
    for c in started:
        c.wait_send()
    b_copy.wait()
    grad_copy.wait()
    a_copy.wait()


def finish(
    factor, grad_hbm, full_a_hbm, full_b_hbm, wdown_ref, gatoms_hbm, gwa_hbm, gwd_hbm, gwt_hbm, gwb_hbm,
    full_a, full_b, grad, gwa, gwd, gwt, gwb, sem,
):
    copies = []

    def copy(src, dst):
        c = pltpu.make_async_copy(src, dst, sem.at[len(copies)])
        c.start()
        copies.append(c)
        return c

    loads_b = [copy(full_b_hbm.at[pl.ds(16 * i, 16)], full_b.at[pl.ds(16 * i, 16)]) for i in range(2)]
    loads_a = [copy(full_a_hbm.at[pl.ds(16 * i, 16)], full_a.at[pl.ds(16 * i, 16)]) for i in range(2)]
    through = copy(grad_hbm, grad)
    loaded = len(copies)

    def rows_of(full, s, part):
        return jnp.concatenate([full[s + c, part].astype(F32) for c in range(4)], axis=1)

    for i in range(2):
        loads_b[i].wait()
        for r in range(4 * i, 4 * i + 4):
            gwb[64 * r : 64 * (r + 1)] = rows_of(full_b, 4 * r, slice(0, 64)) * factor
        copy(gwb.at[pl.ds(256 * i, 256)], gwb_hbm.at[pl.ds(256 * i, 256)])
    for c in loads_a:
        c.wait()
    back = jnp.concatenate([rows_of(full_a, 16 + 4 * r, slice(80, 96)) for r in range(4)], axis=0)
    back = tn(back.astype(BF), wdown_ref[...])
    for i in range(2):
        for r in range(4 * i, 4 * i + 4):
            main = rows_of(full_a, 4 * r, slice(0, 64))
            gwa[64 * r : 64 * (r + 1)] = (main + back[64 * r : 64 * (r + 1)]) * factor
        copy(gwa.at[pl.ds(256 * i, 256)], gwa_hbm.at[pl.ds(256 * i, 256)])
    for r in range(4):
        gwt[16 * r : 16 * (r + 1)] = rows_of(full_a, 4 * r, slice(64, 80)) * factor
        gwd[16 * r : 16 * (r + 1)] = rows_of(full_a, 4 * r, slice(80, 96)) * factor
    copy(gwt, gwt_hbm)
    copy(gwd, gwd_hbm)
    through.wait()
    copy(grad, gatoms_hbm)
    for c in copies[loaded:]:
        c.wait()


def per_device(
    slabs, groups,
    atoms, messages, edge_src, edge_dst, trip_in, trip_out, trip_basis, edge_count, trip_count,
    w_a, w_down, w_t, w_b, cotangent,
):
    dims = dims_of(slabs)
    Y, ZH, X = dims
    XY, Z = X * Y, 2 * ZH
    nb, tile = 16 // XY, 64 // Z
    transfers = 40 + 7 * (XY - 1) + 5 * (Z - 1)
    vmem = pl.BlockSpec(memory_space=pltpu.VMEM)
    hbm = pl.BlockSpec(memory_space=pl.ANY)
    index = [a.reshape(16, 128) for a in (edge_src, edge_dst, trip_in, trip_out)]
    w_down = w_down.T
    V = pltpu.VMEM
    full_a, full_b, grad = pl.pallas_call(
        functools.partial(kernel, dims),
        out_shape=(
            jax.ShapeDtypeStruct((32, 96, 128), BF),
            jax.ShapeDtypeStruct((32, 64, 128), BF),
            jax.ShapeDtypeStruct((OWN, WIDTH), BF),
        ),
        in_specs=[vmem] * 8 + [hbm] * 6,
        out_specs=(hbm, hbm, hbm),
        scratch_shapes=[
            V((4, OWN, WIDTH), BF), V((4, OWN, WIDTH), BF), V((4, OWN, WIDTH), BF),
            V((SLOTS, WIDTH), BF), V((DT, SLOTS), BF), V((512, WIDTH), BF), V((512, WIDTH), BF),
            V((SLOTS, WIDTH), BF), V((SLOTS, WIDTH), F32), V((SLOTS, WIDTH), BF),
            V((SLOTS, 128), jnp.int32), V((SLOTS, 128), jnp.int32),
            V((SLOTS, 128), jnp.int32), V((SLOTS, 128), jnp.int32),
            V((8, SLOTS), jnp.int32), V((SLOTS, 128), F32), V((128, WIDTH), BF), V((128, WIDTH), BF),
            V((SLOTS, 128), BF), V((LO, WIDTH), BF), V((LO, WIDTH), F32), V((SLOTS, 128), BF),
            V((2, 2, ROWS, WIDTH), BF), V((2, ROWS, WIDTH), BF), V((ROWS, WIDTH), BF), V((ROWS, WIDTH), BF),
            V((OWN, WIDTH), BF),
            V((2, 2, ROWS, 128), BF), V((2, ROWS, 128), BF), V((OWN, 128), BF), V((OWN, 128), BF),
            V((OWN, WIDTH), BF), V((2, GH, WIDTH), BF), V((OWN, 128), BF), V((2, GH, 128), BF),
            V((512, WIDTH), F32), V((512, WIDTH), F32), V((128, WIDTH), F32), V((128, WIDTH), F32),
            V((128, WIDTH), F32),
            V((SLOTS, WIDTH), BF), V((SLOTS, WIDTH), F32),
            V((32, 64, 128), BF), V((16, 64, 128), BF), V((16, 64, 128), BF), V((XY - 1, nb, 64, 128), BF),
            V((nb, 64, 128), F32), V((Z - 1, nb, tile, 128), F32), V((nb, 64, 128), F32), V((32, 64, 128), BF),
            V((32, 80, 128), BF), V((16, 80, 128), BF), V((16, 80, 128), BF), V((XY - 1, nb, 80, 128), BF),
            V((nb, 64, 128), F32), V((Z - 1, nb, tile, 128), F32), V((nb, 64, 128), F32), V((32, 96, 128), BF),
            V((32, 16, 128), BF), V((16, 16, 128), BF), V((16, 16, 128), BF), V((XY - 1, nb, 16, 128), BF),
            V((nb, 32, 128), BF), V((Z, nb, 32, 128), BF),
            pltpu.SemaphoreType.DMA((transfers,)), pltpu.SemaphoreType.DMA((transfers,)),
            pltpu.SemaphoreType.DMA((9,)),
        ],
        compiler_params=pltpu.CompilerParams(
            collective_id=0, has_side_effects=True, vmem_limit_bytes=60 * 1024 * 1024
        ),
    )(
        edge_count.reshape(1, 1), trip_count.reshape(1, 1), *index, w_down, w_t,
        atoms, cotangent, messages, trip_basis.T, w_a, w_b,
    )
    factor = 1.0 / math.sqrt(OWN * groups * slabs)
    grad, gwa, gwd, gwt, gwb = pl.pallas_call(
        functools.partial(finish, factor),
        out_shape=(
            jax.ShapeDtypeStruct((OWN, WIDTH), BF),
            jax.ShapeDtypeStruct((512, WIDTH), F32),
            jax.ShapeDtypeStruct((DT, WIDTH), F32),
            jax.ShapeDtypeStruct((DT, WIDTH), F32),
            jax.ShapeDtypeStruct((512, WIDTH), F32),
        ),
        in_specs=[hbm, hbm, hbm, vmem],
        out_specs=(hbm,) * 5,
        scratch_shapes=[
            V((32, 96, 128), BF), V((32, 64, 128), BF), V((OWN, WIDTH), BF), V((512, WIDTH), F32),
            V((DT, WIDTH), F32), V((DT, WIDTH), F32), V((512, WIDTH), F32), pltpu.SemaphoreType.DMA((12,)),
        ],
        compiler_params=pltpu.CompilerParams(vmem_limit_bytes=60 * 1024 * 1024),
    )(grad, full_a, full_b, w_down)
    return grad, gwa, gwd.T, gwt, gwb


def solution(mesh):
    both = P(("dom", "gp"))
    rows = P(("dom", "gp"), None)
    in_specs = (rows, rows, both, both, both, both, rows, both, both, P(), P(), P(), P(), rows)
    out_specs = (rows, P(), P(), P(), P())
    return jax.shard_map(
        functools.partial(per_device, mesh.shape["dom"], mesh.shape["gp"]),
        mesh=mesh, in_specs=in_specs, out_specs=out_specs, check_vma=False,
    )
```

```python
import functools
import math

import jax
import jax.numpy as jnp
from jax import lax
from jax.experimental import pallas as pl
from jax.experimental.pallas import tpu as pltpu
from jax.sharding import PartitionSpec as P

BF = jnp.bfloat16
F32 = jnp.float32
MESH = pl.DeviceIdType.MESH
GH = 128
OWN = 256
SLOTS = 2048
WIDTH = 512
DT = 64
LO = 256
BLK = 512


def dims_of(slabs):
    return {64: (4, 4, 4), 4: (1, 1, 4), 2: (1, 1, 2)}[slabs]


def nn(a, b):
    return lax.dot_general(a, b, (((1,), (0,)), ((), ())), preferred_element_type=F32)


def nt(a, b):
    return lax.dot_general(a, b, (((1,), (1,)), ((), ())), preferred_element_type=F32)


def tn(a, b):
    return lax.dot_general(a, b, (((0,), (0,)), ((), ())), preferred_element_type=F32)


def lanes(shape):
    return lax.broadcasted_iota(jnp.int32, shape, len(shape) - 1)


def pick_columns(index, first, width):
    lane = lanes(index.shape)
    local = index - first
    return jnp.concatenate(
        [jnp.where(local == lane + 128 * j, 1.0, 0.0).astype(BF) for j in range(width // 128)], axis=1
    )


def pick_rows(index, first, height):
    shape = (height, index.shape[1])
    row = lax.broadcasted_iota(jnp.int32, shape, 0)
    return jnp.where(row == jnp.broadcast_to(index - first, shape), 1.0, 0.0).astype(BF)


def table_row(src):
    up = src - 1536
    lower = 4 * OWN + ((src >> 7) << 8) + (src & 127)
    upper = 4 * OWN + ((up >> 7) << 8) + GH + (up & 127)
    return jnp.where(src < 512, lower, jnp.where(src < 1536, src - 512, upper))


def kernel(
    dims,
    ecnt_ref, tcnt_ref, src_ref, dst_ref, tin_ref, tout_ref, wdown_ref, wt_ref,
    atoms_hbm, cot_hbm, msg_hbm, basis_hbm, wa_hbm, wb_hbm,
    full_a_out, full_b_out, grad_out,
    mid, rim, cots, msg, basis, wa, wb, picked, inc, dinc,
    src_col, dst_col, tin_col, tout_col, rows, basis2, wdown2, wt2,
    down, dn, acc_s, sm,
    dt_sib, dt, rd, ed, re, grad, rims_out, rims_in,
    acc_wa, acc_wb, acc_wt, acc_wd, acc_wx, picked_cot, slope,
    pieces_b, rc_b, half_b, rx_b, rz_b, full_b,
    pieces_a, rc_a, half_a, rx_a, rz_a, full_a,
    late, rc_l, half_l, rx_l, rz_l,
    send, recv, local_sem,
):
    Y, ZH, X = dims
    XY = X * Y
    Z = 2 * ZH
    nb = 16 // XY
    dom = lax.axis_index("dom")
    gp = lax.axis_index("gp")
    slabs = Y * ZH * X
    x = lax.rem(dom, X)
    zh = lax.rem(lax.div(dom, X), ZH)
    y = lax.div(dom, X * ZH)
    core = lax.rem(gp, 2)
    zl = lax.div(gp, 2)
    z = zh * 2 + zl

    sib = {"dom": dom, "gp": zl * 2 + (1 - core)}
    zpart = {"dom": dom, "gp": (1 - zl) * 2 + core}
    kz = (1 - zl) * 2 + core
    above = {"dom": lax.rem(dom + 1, slabs), "gp": gp}
    below = {"dom": lax.rem(dom + slabs - 1, slabs), "gp": gp}
    xy_peers = []
    for j in range(1, XY):
        px = lax.rem(x + j // Y, X)
        py = lax.rem(y + j % Y, Y)
        xy_peers.append((px * Y + py, {"dom": (py * ZH + zh) * X + px, "gp": gp}))
    z_peers = []
    for j in range(1, Z):
        pz = lax.rem(z + j, Z)
        z_peers.append({"dom": (y * ZH + lax.div(pz, 2)) * X + x, "gp": lax.rem(pz, 2) * 2 + core})

    barrier = pltpu.get_barrier_semaphore()
    others = [sib, above, below] + [d for _, d in xy_peers] + z_peers
    for d in others:
        pl.semaphore_signal(barrier, inc=1, device_id=d, device_id_type=MESH)

    count = [0]
    started = []

    def remote(src, dst, device):
        i = count[0]
        count[0] += 1
        c = pltpu.make_async_remote_copy(
            src_ref=src, dst_ref=dst, send_sem=send.at[i], recv_sem=recv.at[i],
            device_id=device, device_id_type=MESH,
        )
        c.start()
        started.append(c)
        return c

    local = []
    for i, (src, dst) in enumerate(
        (
            (atoms_hbm, mid.at[gp]), (cot_hbm, cots.at[gp]), (basis_hbm, basis),
            (wa_hbm, wa), (msg_hbm, msg), (wb_hbm, wb),
        )
    ):
        c = pltpu.make_async_copy(src, dst, local_sem.at[i])
        c.start()
        local.append(c)
    atoms_in, cot_in, basis_in, wa_in, msg_in, wb_in = local

    pl.semaphore_wait(barrier, len(others))

    low = pl.ds(0, GH)
    high = pl.ds(GH, GH)
    to_above = remote(atoms_hbm.at[high], rim.at[gp, low], above)
    to_below = remote(atoms_hbm.at[low], rim.at[gp, high], below)
    to_z = remote(atoms_hbm, mid.at[gp], zpart)
    to_sib = remote(atoms_hbm, mid.at[gp], sib)

    edges = ecnt_ref[...]
    trips = tcnt_ref[...]
    for n, (ref, col) in enumerate(
        ((src_ref, src_col), (dst_ref, dst_col), (tin_ref, tin_col), (tout_ref, tout_col))
    ):
        flat = ref[...]
        if n == 0:
            flat = table_row(flat)
        for j in range(SLOTS // 128):
            line = flat[j : j + 1]
            rows[n : n + 1, 128 * j : 128 * (j + 1)] = line
            col[128 * j : 128 * (j + 1)] = jnp.transpose(jnp.broadcast_to(line, (128, 128)))
    wdown2[...] = jnp.concatenate([wdown_ref[...], wdown_ref[...]], axis=0)
    wt2[...] = jnp.concatenate([wt_ref[...], wt_ref[...]], axis=0)
    basis_in.wait()
    twice = jnp.where(
        lax.broadcasted_iota(jnp.int32, (DT, 128), 0) == (lanes((DT, 128)) & (DT - 1)), 1.0, 0.0
    ).astype(BF)
    valid = lax.broadcasted_iota(jnp.int32, (SLOTS, 128), 0) < jnp.broadcast_to(trips, (SLOTS, 128))
    basis2[...] = jnp.where(valid, tn(basis[...], twice), 0.0)

    atoms_in.wait()
    to_sib.wait_recv()
    to_above.wait_recv()
    z_low = remote(rim.at[gp, low], rim.at[gp, low], zpart)
    s_low = remote(rim.at[gp, low], rim.at[gp, low], sib)
    to_below.wait_recv()
    z_high = remote(rim.at[gp, high], rim.at[gp, high], zpart)
    s_high = remote(rim.at[gp, high], rim.at[gp, high], sib)
    z_cot = remote(cot_hbm, cots.at[gp], zpart)
    s_cot = remote(cot_hbm, cots.at[gp], sib)
    to_z.wait_recv()
    f_mid = remote(mid.at[kz], mid.at[kz], sib)
    f_mid.wait_recv()

    def block(b):
        return pl.ds(pl.multiple_of(b * BLK, BLK), BLK)

    def gather(index, first, source):
        got = nn(pick_columns(index, first, OWN), source[0])
        for k in range(1, 4):
            got = got + nn(pick_columns(index, first + k * OWN, OWN), source[k])
        return got

    def edge_own(b, carry):
        picked[block(b)] = gather(src_col[block(b)], 0, mid).astype(BF)
        return carry

    lax.fori_loop(0, SLOTS // BLK, edge_own, 0)

    z_low.wait_recv()
    f_low = remote(rim.at[kz, low], rim.at[kz, low], sib)
    z_high.wait_recv()
    f_high = remote(rim.at[kz, high], rim.at[kz, high], sib)
    for c in (s_low, s_high, f_low, f_high):
        c.wait_recv()
    wa_in.wait()
    msg_in.wait()

    def row_mask(b, width):
        shape = (BLK, width)
        return lax.broadcasted_iota(jnp.int32, shape, 0) < jnp.broadcast_to(edges - b * BLK, shape)

    def edge_in(b, carry):
        at = block(b)
        got = (picked[at].astype(F32) + gather(src_col[at], 4 * OWN, rim)).astype(BF)
        picked[at] = got
        proj = nn(got, wa[...]).astype(BF).astype(F32)
        value = jnp.where(row_mask(b, WIDTH), proj + msg[at].astype(F32), 0.0)
        inc[at] = value
        down[at] = nt(value.astype(BF), wdown2[...]).astype(BF)
        return carry

    lax.fori_loop(0, SLOTS // BLK, edge_in, 0)
    z_cot.wait_recv()
    f_cot = remote(cots.at[kz], cots.at[kz], sib)

    def pack(source):
        first = lanes((LO, 128)) < DT
        for j in range(4):
            a = source[2 * j * LO : (2 * j + 1) * LO].astype(F32)
            b = source[(2 * j + 1) * LO : (2 * j + 2) * LO].astype(F32)
            dn[:, 128 * j : 128 * (j + 1)] = jnp.where(first, a, b).astype(BF)

    def unpack():
        first = lanes((LO, 128)) < DT
        for j in range(4):
            v = acc_s[:, 128 * j : 128 * (j + 1)]
            sm[2 * j * LO : (2 * j + 1) * LO] = jnp.where(first, v, 0.0).astype(BF)
            sm[(2 * j + 1) * LO : (2 * j + 2) * LO] = jnp.where(first, 0.0, v).astype(BF)

    def triplets(from_col, to_col, to_row, between=lambda: None):
        half_lane = jnp.where(lanes((BLK, 128)) < DT, 0, 1)
        acc_s[...] = jnp.zeros_like(acc_s)

        def body(b, carry):
            at = block(b)
            frm = from_col[at]
            to = to_col[at]
            got = nn(pick_columns(frm & (LO - 1), 0, LO), dn[...])
            frm_hi = frm >> 8
            to_hi = to >> 8
            value = jnp.where(frm_hi == half_lane, got[:, 0:128], 0.0)
            for j in range(1, 4):
                value = value + jnp.where(
                    frm_hi == half_lane + 2 * j, got[:, 128 * j : 128 * (j + 1)], 0.0
                )
            value = value + pltpu.roll(value, DT, 1)
            value = value * basis2[at]
            spread = jnp.concatenate(
                [jnp.where(to_hi == half_lane + 2 * j, value, 0.0).astype(BF) for j in range(4)], axis=1
            )
            line = rows[to_row : to_row + 1, block(b)]
            acc_s[...] += nn(pick_rows(line & (LO - 1), 0, LO), spread)
            return carry

        lax.fori_loop(0, 2, body, 0)
        result = between()
        lax.fori_loop(2, SLOTS // BLK, body, 0)
        return result

    pack(down)
    triplets(tin_col, tout_col, 3)
    unpack()
    cot_in.wait()
    wb_in.wait()
    s_cot.wait_recv()
    f_cot.wait_recv()

    for acc in (acc_wa, acc_wb, acc_wt, acc_wd, acc_wx):
        acc[...] = jnp.zeros_like(acc)

    not_mine = pl.ds((1 - core) * 16, 16)
    mine = pl.ds(core * 16, 16)
    own_s = x * Y + y
    own_nb = pl.ds(own_s * nb, nb)
    own_piece = pl.ds(core * 16 + own_s * nb, nb)

    def reduce_core(copy, pieces, received, half, got):
        copy.wait_recv()
        half[...] = (pieces[mine].astype(F32) + received[...].astype(F32)).astype(BF)
        return [
            remote(half.at[pl.ds(s * nb, nb)], got.at[j], d) for j, (s, d) in enumerate(xy_peers)
        ]

    def sum_xy(copies, half, got):
        for c in copies:
            c.wait_recv()
        total = half[own_nb].astype(F32)
        for j in range(XY - 1):
            total = total + got[j].astype(F32)
        return total

    def send_z(own, got):
        got[0] = own.astype(BF)
        return [remote(got.at[0], got.at[j + 1], d) for j, d in enumerate(z_peers)]

    def sum_z(copies, got):
        for c in copies:
            c.wait_recv()
        total = got[lax.rem(Z - z, Z)].astype(F32)
        for j in range(1, Z):
            total = total + got[lax.rem(j + Z - z, Z)].astype(F32)
        return total.astype(BF)

    def spread(full):
        own = full.at[own_piece]
        return [remote(own, own, d) for _, d in xy_peers], [remote(own, own, sib)]

    def forward(copies, to_core, full):
        for j, c in enumerate(copies):
            c.wait_recv()
            px = lax.rem(x + X - (j + 1) // Y, X)
            py = lax.rem(y + Y - (j + 1) % Y, Y)
            piece = full.at[pl.ds(core * 16 + (px * Y + py) * nb, nb)]
            to_core.append(remote(piece, piece, sib))

    def fold(acc, r, cols):
        return (acc[16 * r : 16 * (r + 1), cols] + acc[DT + 16 * r : DT + 16 * (r + 1), cols]).astype(BF)

    def edge_mid(b, carry):
        at = block(b)
        mask = row_mask(b, WIDTH)
        cot = gather(dst_col[at], 0, cots).astype(BF)
        picked_cot[at] = cot
        pre = inc[at] + nn(sm[at], wt2[...])
        sig = jax.nn.sigmoid(pre)
        out = jnp.where(mask, pre * sig, 0.0).astype(BF)
        slope[at] = jnp.where(mask, sig * (1.0 + pre * (1.0 - sig)), 0.0)
        acc_wb[...] += tn(out, cot)
        return carry

    lax.fori_loop(0, SLOTS // BLK, edge_mid, 0)
    for s in range(32):
        r, cols = s // 4, slice(128 * (s % 4), 128 * (s % 4 + 1))
        pieces_b[s] = acc_wb[64 * r : 64 * (r + 1), cols].astype(BF)
    b_core = remote(pieces_b.at[not_mine], rc_b, sib)

    def edge_grad(b, carry):
        at = block(b)
        grad = nt(picked_cot[at], wb[...]) * slope[at]
        slope[at] = grad
        grad = grad.astype(BF)
        acc_wa[...] += tn(picked[at], grad)
        acc_wt[...] += tn(sm[at], grad)
        down[at] = nt(grad, wt2[...]).astype(BF)
        return carry

    lax.fori_loop(0, 2, edge_grad, 0)
    b_xy = reduce_core(b_core, pieces_b, rc_b, half_b, rx_b)
    lax.fori_loop(2, SLOTS // BLK, edge_grad, 0)

    for s in range(32):
        r, cols = s // 4, slice(128 * (s % 4), 128 * (s % 4 + 1))
        pieces_a[s, 0:64] = acc_wa[64 * r : 64 * (r + 1), cols].astype(BF)
        pieces_a[s, 64:80] = fold(acc_wt, r, cols) if s < 16 else jnp.zeros((16, 128), BF)
    a_core = remote(pieces_a.at[not_mine], rc_a, sib)

    pack(down)
    a_xy = triplets(
        tout_col, tin_col, 2, lambda: reduce_core(a_core, pieces_a, rc_a, half_a, rx_a)
    )
    unpack()

    def edge_out(b, carry):
        at = block(b)
        mask = row_mask(b, 128)
        back = jnp.where(mask, sm[at].astype(F32), 0.0).astype(BF)
        dinc[at] = (slope[at] + nn(back, wdown2[...])).astype(BF)
        acc_wd[...] += tn(back, inc[at].astype(BF))
        acc_wx[...] += tn(back, picked[at])
        return carry

    lax.fori_loop(0, SLOTS // BLK, edge_out, 0)
    for s in range(32):
        r, c = (s % 16) // 4, s % 4
        late[s] = fold(acc_wd if s < 16 else acc_wx, r, slice(128 * c, 128 * (c + 1)))
    l_core = remote(late.at[not_mine], rc_l, sib)

    def table_grad(owner, part, out):
        first = (4 + owner) * OWN if part == 0 else owner * OWN
        total = None
        for b in range(SLOTS // BLK):
            cols = slice(BLK * b, BLK * (b + 1))
            line = rows[0:1, cols]
            choice = jnp.concatenate(
                [pick_rows(line, first, OWN), pick_rows(line, first + 2 * OWN, OWN)], axis=0
            )
            term = nn(choice, dinc[cols])
            total = term if total is None else total + term
        total = total.astype(BF)
        out[part, 0] = total[0:OWN]
        out[part, 1] = total[OWN:]

    def reduce_slot(part):
        ed[part] = (dt[part, 1 - zl].astype(F32) + rd[part, 1 - zl].astype(F32)).astype(BF)
        return remote(ed.at[part], re.at[part], zpart)

    def slot_sum(part):
        return dt[part, zl].astype(F32) + rd[part, zl].astype(F32) + re[part].astype(F32)

    table_grad(1 - core, 0, dt_sib)
    rim_core = remote(dt_sib.at[0], rd.at[0], sib)
    rz = send_z(sum_xy(b_xy, half_b, rx_b), rz_b)
    table_grad(core, 0, dt)
    l_xy = reduce_core(l_core, late, rc_l, half_l, rx_l)
    rim_core.wait_recv()
    rim_z = reduce_slot(0)
    table_grad(1 - core, 1, dt_sib)
    mid_core = remote(dt_sib.at[1], rd.at[1], sib)
    a_z = send_z(sum_xy(a_xy, half_a, rx_a), rz_a)
    table_grad(core, 1, dt)
    full_b[own_piece] = sum_z(rz, rz_b)
    g_bxy, g_bcore = spread(full_b)
    l_z = send_z(sum_xy(l_xy, half_l, rx_l), rz_l)
    mid_core.wait_recv()
    mid_z = reduce_slot(1)

    rim_z.wait_recv()
    rims_out[...] = slot_sum(0).astype(BF)
    to_tails = remote(rims_out.at[low], rims_in.at[0], below)
    to_heads = remote(rims_out.at[high], rims_in.at[1], above)

    full_a[own_piece, 0:80] = sum_z(a_z, rz_a)
    full_a[own_piece, 80:96] = sum_z(l_z, rz_l)
    g_axy, g_acore = spread(full_a)
    forward(g_bxy, g_bcore, full_b)
    for c in g_bcore:
        c.wait_recv()
    b_copy = pltpu.make_async_copy(full_b, full_b_out, local_sem.at[8])
    b_copy.start()
    forward(g_axy, g_acore, full_a)

    mid_z.wait_recv()
    to_tails.wait_recv()
    to_heads.wait_recv()
    dproj = slot_sum(1) + jnp.concatenate([rims_in[1].astype(F32), rims_in[0].astype(F32)], axis=0)
    coarse = dproj.astype(BF)
    fine = (dproj - coarse.astype(F32)).astype(BF)
    grad[...] = (nt(coarse, wa[...]) + nt(fine, wa[...])).astype(BF)
    grad_copy = pltpu.make_async_copy(grad, grad_out, local_sem.at[6])
    grad_copy.start()

    for c in g_acore:
        c.wait_recv()
    a_copy = pltpu.make_async_copy(full_a, full_a_out, local_sem.at[7])
    a_copy.start()
    for c in started:
        c.wait_send()
    b_copy.wait()
    grad_copy.wait()
    a_copy.wait()


def finish(
    factor, grad_hbm, full_a_hbm, full_b_hbm, wdown_ref, gatoms_hbm, gwa_hbm, gwd_hbm, gwt_hbm, gwb_hbm,
    full_a, full_b, grad, gwa, gwd, gwt, gwb, sem,
):
    copies = []

    def copy(src, dst):
        c = pltpu.make_async_copy(src, dst, sem.at[len(copies)])
        c.start()
        copies.append(c)
        return c

    loads_b = [copy(full_b_hbm.at[pl.ds(16 * i, 16)], full_b.at[pl.ds(16 * i, 16)]) for i in range(2)]
    loads_a = [copy(full_a_hbm.at[pl.ds(16 * i, 16)], full_a.at[pl.ds(16 * i, 16)]) for i in range(2)]
    through = copy(grad_hbm, grad)
    loaded = len(copies)

    def rows_of(full, s, part):
        return jnp.concatenate([full[s + c, part].astype(F32) for c in range(4)], axis=1)

    for i in range(2):
        loads_b[i].wait()
        for r in range(4 * i, 4 * i + 4):
            gwb[64 * r : 64 * (r + 1)] = rows_of(full_b, 4 * r, slice(0, 64)) * factor
        copy(gwb.at[pl.ds(256 * i, 256)], gwb_hbm.at[pl.ds(256 * i, 256)])
    for c in loads_a:
        c.wait()
    back = jnp.concatenate([rows_of(full_a, 16 + 4 * r, slice(80, 96)) for r in range(4)], axis=0)
    back = tn(back.astype(BF), wdown_ref[...])
    for i in range(2):
        for r in range(4 * i, 4 * i + 4):
            main = rows_of(full_a, 4 * r, slice(0, 64))
            gwa[64 * r : 64 * (r + 1)] = (main + back[64 * r : 64 * (r + 1)]) * factor
        copy(gwa.at[pl.ds(256 * i, 256)], gwa_hbm.at[pl.ds(256 * i, 256)])
    for r in range(4):
        gwt[16 * r : 16 * (r + 1)] = rows_of(full_a, 4 * r, slice(64, 80)) * factor
        gwd[16 * r : 16 * (r + 1)] = rows_of(full_a, 4 * r, slice(80, 96)) * factor
    copy(gwt, gwt_hbm)
    copy(gwd, gwd_hbm)
    through.wait()
    copy(grad, gatoms_hbm)
    for c in copies[loaded:]:
        c.wait()


def per_device(
    slabs, groups,
    atoms, messages, edge_src, edge_dst, trip_in, trip_out, trip_basis, edge_count, trip_count,
    w_a, w_down, w_t, w_b, cotangent,
):
    dims = dims_of(slabs)
    Y, ZH, X = dims
    XY, Z = X * Y, 2 * ZH
    nb = 16 // XY
    transfers = 40 + 7 * (XY - 1) + 5 * (Z - 1)
    vmem = pl.BlockSpec(memory_space=pltpu.VMEM)
    hbm = pl.BlockSpec(memory_space=pl.ANY)
    index = [a.reshape(16, 128) for a in (edge_src, edge_dst, trip_in, trip_out)]
    w_down = w_down.T
    V = pltpu.VMEM
    full_a, full_b, grad = pl.pallas_call(
        functools.partial(kernel, dims),
        out_shape=(
            jax.ShapeDtypeStruct((32, 96, 128), BF),
            jax.ShapeDtypeStruct((32, 64, 128), BF),
            jax.ShapeDtypeStruct((OWN, WIDTH), BF),
        ),
        in_specs=[vmem] * 8 + [hbm] * 6,
        out_specs=(hbm, hbm, hbm),
        scratch_shapes=[
            V((4, OWN, WIDTH), BF), V((4, OWN, WIDTH), BF), V((4, OWN, WIDTH), BF),
            V((SLOTS, WIDTH), BF), V((DT, SLOTS), BF), V((512, WIDTH), BF), V((512, WIDTH), BF),
            V((SLOTS, WIDTH), BF), V((SLOTS, WIDTH), F32), V((SLOTS, WIDTH), BF),
            V((SLOTS, 128), jnp.int32), V((SLOTS, 128), jnp.int32),
            V((SLOTS, 128), jnp.int32), V((SLOTS, 128), jnp.int32),
            V((8, SLOTS), jnp.int32), V((SLOTS, 128), F32), V((128, WIDTH), BF), V((128, WIDTH), BF),
            V((SLOTS, 128), BF), V((LO, WIDTH), BF), V((LO, WIDTH), F32), V((SLOTS, 128), BF),
            V((2, 2, OWN, WIDTH), BF), V((2, 2, OWN, WIDTH), BF), V((2, 2, OWN, WIDTH), BF),
            V((2, OWN, WIDTH), BF), V((2, OWN, WIDTH), BF), V((OWN, WIDTH), BF),
            V((OWN, WIDTH), BF), V((2, GH, WIDTH), BF),
            V((512, WIDTH), F32), V((512, WIDTH), F32), V((128, WIDTH), F32), V((128, WIDTH), F32),
            V((128, WIDTH), F32),
            V((SLOTS, WIDTH), BF), V((SLOTS, WIDTH), F32),
            V((32, 64, 128), BF), V((16, 64, 128), BF), V((16, 64, 128), BF), V((XY - 1, nb, 64, 128), BF),
            V((Z, nb, 64, 128), BF), V((32, 64, 128), BF),
            V((32, 80, 128), BF), V((16, 80, 128), BF), V((16, 80, 128), BF), V((XY - 1, nb, 80, 128), BF),
            V((Z, nb, 80, 128), BF), V((32, 96, 128), BF),
            V((32, 16, 128), BF), V((16, 16, 128), BF), V((16, 16, 128), BF), V((XY - 1, nb, 16, 128), BF),
            V((Z, nb, 16, 128), BF),
            pltpu.SemaphoreType.DMA((transfers,)), pltpu.SemaphoreType.DMA((transfers,)),
            pltpu.SemaphoreType.DMA((9,)),
        ],
        compiler_params=pltpu.CompilerParams(
            collective_id=0, has_side_effects=True, vmem_limit_bytes=60 * 1024 * 1024
        ),
    )(
        edge_count.reshape(1, 1), trip_count.reshape(1, 1), *index, w_down, w_t,
        atoms, cotangent, messages, trip_basis.T, w_a, w_b,
    )
    factor = 1.0 / math.sqrt(OWN * groups * slabs)
    grad, gwa, gwd, gwt, gwb = pl.pallas_call(
        functools.partial(finish, factor),
        out_shape=(
            jax.ShapeDtypeStruct((OWN, WIDTH), BF),
            jax.ShapeDtypeStruct((512, WIDTH), F32),
            jax.ShapeDtypeStruct((DT, WIDTH), F32),
            jax.ShapeDtypeStruct((DT, WIDTH), F32),
            jax.ShapeDtypeStruct((512, WIDTH), F32),
        ),
        in_specs=[hbm, hbm, hbm, vmem],
        out_specs=(hbm,) * 5,
        scratch_shapes=[
            V((32, 96, 128), BF), V((32, 64, 128), BF), V((OWN, WIDTH), BF), V((512, WIDTH), F32),
            V((DT, WIDTH), F32), V((DT, WIDTH), F32), V((512, WIDTH), F32), pltpu.SemaphoreType.DMA((12,)),
        ],
        compiler_params=pltpu.CompilerParams(vmem_limit_bytes=60 * 1024 * 1024),
    )(grad, full_a, full_b, w_down)
    return grad, gwa, gwd.T, gwt, gwb


def solution(mesh):
    both = P(("dom", "gp"))
    rows = P(("dom", "gp"), None)
    in_specs = (rows, rows, both, both, both, both, rows, both, both, P(), P(), P(), P(), rows)
    out_specs = (rows, P(), P(), P(), P())
    return jax.shard_map(
        functools.partial(per_device, mesh.shape["dom"], mesh.shape["gp"]),
        mesh=mesh, in_specs=in_specs, out_specs=out_specs, check_vma=False,
    )
```

```python
import functools
import math

import jax
import jax.numpy as jnp
from jax import lax
from jax.experimental import pallas as pl
from jax.experimental.pallas import tpu as pltpu
from jax.sharding import PartitionSpec as P

BF = jnp.bfloat16
F32 = jnp.float32
MESH = pl.DeviceIdType.MESH
GH = 128
OWN = 256
SLOTS = 2048
WIDTH = 512
DT = 64
LO = 256
BLK = 512


def dims_of(slabs):
    return {64: (4, 4, 4), 4: (1, 1, 4), 2: (1, 1, 2)}[slabs]


def nn(a, b):
    return lax.dot_general(a, b, (((1,), (0,)), ((), ())), preferred_element_type=F32)


def nt(a, b):
    return lax.dot_general(a, b, (((1,), (1,)), ((), ())), preferred_element_type=F32)


def tn(a, b):
    return lax.dot_general(a, b, (((0,), (0,)), ((), ())), preferred_element_type=F32)


def lanes(shape):
    return lax.broadcasted_iota(jnp.int32, shape, len(shape) - 1)


def pick_columns(index, first, width):
    lane = lanes(index.shape)
    local = index - first
    return jnp.concatenate(
        [jnp.where(local == lane + 128 * j, 1.0, 0.0).astype(BF) for j in range(width // 128)], axis=1
    )


def pick_rows(index, first, height):
    shape = (height, index.shape[1])
    row = lax.broadcasted_iota(jnp.int32, shape, 0)
    return jnp.where(row == jnp.broadcast_to(index - first, shape), 1.0, 0.0).astype(BF)


def table_row(src):
    up = src - 1536
    lower = 4 * OWN + ((src >> 7) << 8) + (src & 127)
    upper = 4 * OWN + ((up >> 7) << 8) + GH + (up & 127)
    return jnp.where(src < 512, lower, jnp.where(src < 1536, src - 512, upper))


def kernel(
    dims,
    ecnt_ref, tcnt_ref, src_ref, dst_ref, tin_ref, tout_ref, wdown_ref, wt_ref,
    atoms_hbm, cot_hbm, msg_hbm, basis_hbm, wa_hbm, wb_hbm,
    full_a_out, full_b_out, grad_out,
    mid, rim, cots, msg, basis, wa, wb, picked, inc, dinc,
    src_col, dst_col, tin_col, tout_col, rows, basis2, wdown2, wt2,
    down, dn, acc_s, sm,
    dt_sib, dt, rd, ed, re, grad, rims_out, rims_in,
    nt_sib, ntd, nrd, ned, nre, rims2_out, rims2_in,
    acc_wa, acc_wb, acc_wt, acc_wd, acc_wx, picked_cot, slope,
    pieces_b, rc_b, half_b, rx_b, rz_b, full_b,
    pieces_a, rc_a, half_a, rx_a, rz_a, full_a,
    late, rc_l, half_l, rx_l, rz_l,
    send, recv, local_sem,
):
    Y, ZH, X = dims
    XY = X * Y
    Z = 2 * ZH
    nb = 16 // XY
    dom = lax.axis_index("dom")
    gp = lax.axis_index("gp")
    slabs = Y * ZH * X
    x = lax.rem(dom, X)
    zh = lax.rem(lax.div(dom, X), ZH)
    y = lax.div(dom, X * ZH)
    core = lax.rem(gp, 2)
    zl = lax.div(gp, 2)
    z = zh * 2 + zl

    sib = {"dom": dom, "gp": zl * 2 + (1 - core)}
    zpart = {"dom": dom, "gp": (1 - zl) * 2 + core}
    kz = (1 - zl) * 2 + core
    above = {"dom": lax.rem(dom + 1, slabs), "gp": gp}
    below = {"dom": lax.rem(dom + slabs - 1, slabs), "gp": gp}
    xy_peers = []
    for j in range(1, XY):
        px = lax.rem(x + j // Y, X)
        py = lax.rem(y + j % Y, Y)
        xy_peers.append((px * Y + py, {"dom": (py * ZH + zh) * X + px, "gp": gp}))
    z_peers = []
    for j in range(1, Z):
        pz = lax.rem(z + j, Z)
        z_peers.append({"dom": (y * ZH + lax.div(pz, 2)) * X + x, "gp": lax.rem(pz, 2) * 2 + core})

    barrier = pltpu.get_barrier_semaphore()
    others = [sib, above, below] + [d for _, d in xy_peers] + z_peers
    for d in others:
        pl.semaphore_signal(barrier, inc=1, device_id=d, device_id_type=MESH)

    count = [0]
    started = []

    def remote(src, dst, device):
        i = count[0]
        count[0] += 1
        c = pltpu.make_async_remote_copy(
            src_ref=src, dst_ref=dst, send_sem=send.at[i], recv_sem=recv.at[i],
            device_id=device, device_id_type=MESH,
        )
        c.start()
        started.append(c)
        return c

    local = []
    for i, (src, dst) in enumerate(
        (
            (atoms_hbm, mid.at[gp]), (cot_hbm, cots.at[gp]), (basis_hbm, basis),
            (wa_hbm, wa), (msg_hbm, msg), (wb_hbm, wb),
        )
    ):
        c = pltpu.make_async_copy(src, dst, local_sem.at[i])
        c.start()
        local.append(c)
    atoms_in, cot_in, basis_in, wa_in, msg_in, wb_in = local

    pl.semaphore_wait(barrier, len(others))

    low = pl.ds(0, GH)
    high = pl.ds(GH, GH)
    to_above = remote(atoms_hbm.at[high], rim.at[gp, low], above)
    to_below = remote(atoms_hbm.at[low], rim.at[gp, high], below)
    to_z = remote(atoms_hbm, mid.at[gp], zpart)
    to_sib = remote(atoms_hbm, mid.at[gp], sib)

    edges = ecnt_ref[...]
    trips = tcnt_ref[...]
    for n, (ref, col) in enumerate(
        ((src_ref, src_col), (dst_ref, dst_col), (tin_ref, tin_col), (tout_ref, tout_col))
    ):
        flat = ref[...]
        if n == 0:
            flat = table_row(flat)
        for j in range(SLOTS // 128):
            line = flat[j : j + 1]
            rows[n : n + 1, 128 * j : 128 * (j + 1)] = line
            col[128 * j : 128 * (j + 1)] = jnp.transpose(jnp.broadcast_to(line, (128, 128)))
    wdown2[...] = jnp.concatenate([wdown_ref[...], wdown_ref[...]], axis=0)
    wt2[...] = jnp.concatenate([wt_ref[...], wt_ref[...]], axis=0)
    basis_in.wait()
    twice = jnp.where(
        lax.broadcasted_iota(jnp.int32, (DT, 128), 0) == (lanes((DT, 128)) & (DT - 1)), 1.0, 0.0
    ).astype(BF)
    valid = lax.broadcasted_iota(jnp.int32, (SLOTS, 128), 0) < jnp.broadcast_to(trips, (SLOTS, 128))
    basis2[...] = jnp.where(valid, tn(basis[...], twice), 0.0)

    atoms_in.wait()
    to_sib.wait_recv()
    to_above.wait_recv()
    z_low = remote(rim.at[gp, low], rim.at[gp, low], zpart)
    s_low = remote(rim.at[gp, low], rim.at[gp, low], sib)
    to_below.wait_recv()
    z_high = remote(rim.at[gp, high], rim.at[gp, high], zpart)
    s_high = remote(rim.at[gp, high], rim.at[gp, high], sib)
    s_cot = remote(cot_hbm, cots.at[gp], sib)
    to_z.wait_recv()
    f_mid = remote(mid.at[kz], mid.at[kz], sib)
    f_mid.wait_recv()

    def block(b):
        return pl.ds(pl.multiple_of(b * BLK, BLK), BLK)

    def gather(index, first, source):
        got = nn(pick_columns(index, first, OWN), source[0])
        for k in range(1, 4):
            got = got + nn(pick_columns(index, first + k * OWN, OWN), source[k])
        return got

    def edge_own(b, carry):
        picked[block(b)] = gather(src_col[block(b)], 0, mid).astype(BF)
        return carry

    lax.fori_loop(0, SLOTS // BLK, edge_own, 0)

    z_low.wait_recv()
    f_low = remote(rim.at[kz, low], rim.at[kz, low], sib)
    z_high.wait_recv()
    f_high = remote(rim.at[kz, high], rim.at[kz, high], sib)
    z_cot = remote(cot_hbm, cots.at[gp], zpart)
    for c in (s_low, s_high, f_low, f_high):
        c.wait_recv()
    wa_in.wait()
    msg_in.wait()

    def row_mask(b, width):
        shape = (BLK, width)
        return lax.broadcasted_iota(jnp.int32, shape, 0) < jnp.broadcast_to(edges - b * BLK, shape)

    def edge_in(b, carry):
        at = block(b)
        got = (picked[at].astype(F32) + gather(src_col[at], 4 * OWN, rim)).astype(BF)
        picked[at] = got
        proj = nn(got, wa[...]).astype(BF).astype(F32)
        value = jnp.where(row_mask(b, WIDTH), proj + msg[at].astype(F32), 0.0)
        inc[at] = value
        down[at] = nt(value.astype(BF), wdown2[...]).astype(BF)
        return carry

    lax.fori_loop(0, SLOTS // BLK, edge_in, 0)

    def pack(source):
        first = lanes((LO, 128)) < DT
        for j in range(4):
            a = source[2 * j * LO : (2 * j + 1) * LO].astype(F32)
            b = source[(2 * j + 1) * LO : (2 * j + 2) * LO].astype(F32)
            dn[:, 128 * j : 128 * (j + 1)] = jnp.where(first, a, b).astype(BF)

    def unpack():
        first = lanes((LO, 128)) < DT
        for j in range(4):
            v = acc_s[:, 128 * j : 128 * (j + 1)]
            sm[2 * j * LO : (2 * j + 1) * LO] = jnp.where(first, v, 0.0).astype(BF)
            sm[(2 * j + 1) * LO : (2 * j + 2) * LO] = jnp.where(first, 0.0, v).astype(BF)

    def triplets(from_col, to_col, to_row):
        half_lane = jnp.where(lanes((BLK, 128)) < DT, 0, 1)
        acc_s[...] = jnp.zeros_like(acc_s)

        def body(b, carry):
            at = block(b)
            frm = from_col[at]
            to = to_col[at]
            got = nn(pick_columns(frm & (LO - 1), 0, LO), dn[...])
            frm_hi = frm >> 8
            to_hi = to >> 8
            value = jnp.where(frm_hi == half_lane, got[:, 0:128], 0.0)
            for j in range(1, 4):
                value = value + jnp.where(
                    frm_hi == half_lane + 2 * j, got[:, 128 * j : 128 * (j + 1)], 0.0
                )
            value = value + pltpu.roll(value, DT, 1)
            value = value * basis2[at]
            spread = jnp.concatenate(
                [jnp.where(to_hi == half_lane + 2 * j, value, 0.0).astype(BF) for j in range(4)], axis=1
            )
            line = rows[to_row : to_row + 1, block(b)]
            acc_s[...] += nn(pick_rows(line & (LO - 1), 0, LO), spread)
            return carry

        lax.fori_loop(0, SLOTS // BLK, body, 0)

    pack(down)
    triplets(tin_col, tout_col, 3)
    unpack()
    z_cot.wait_recv()
    f_cot = remote(cots.at[kz], cots.at[kz], sib)
    cot_in.wait()
    wb_in.wait()
    s_cot.wait_recv()
    f_cot.wait_recv()

    for acc in (acc_wa, acc_wb, acc_wt, acc_wd, acc_wx):
        acc[...] = jnp.zeros_like(acc)

    not_mine = pl.ds((1 - core) * 16, 16)
    mine = pl.ds(core * 16, 16)
    own_s = x * Y + y
    own_nb = pl.ds(own_s * nb, nb)
    own_piece = pl.ds(core * 16 + own_s * nb, nb)

    def reduce_core(copy, pieces, received, half, got):
        copy.wait_recv()
        half[...] = (pieces[mine].astype(F32) + received[...].astype(F32)).astype(BF)
        return [
            remote(half.at[pl.ds(s * nb, nb)], got.at[j], d) for j, (s, d) in enumerate(xy_peers)
        ]

    def sum_xy(copies, half, got):
        for c in copies:
            c.wait_recv()
        total = half[own_nb].astype(F32)
        for j in range(XY - 1):
            total = total + got[j].astype(F32)
        return total

    def send_z(own, got):
        got[0] = own.astype(BF)
        return [remote(got.at[0], got.at[j + 1], d) for j, d in enumerate(z_peers)]

    def sum_z(copies, got):
        for c in copies:
            c.wait_recv()
        total = got[lax.rem(Z - z, Z)].astype(F32)
        for j in range(1, Z):
            total = total + got[lax.rem(j + Z - z, Z)].astype(F32)
        return total.astype(BF)

    def spread(full, part):
        own = full.at[own_piece, part]
        return [remote(own, own, d) for _, d in xy_peers], [remote(own, own, sib)]

    def forward(copies, to_core, full, part):
        for j, c in enumerate(copies):
            c.wait_recv()
            px = lax.rem(x + X - (j + 1) // Y, X)
            py = lax.rem(y + Y - (j + 1) % Y, Y)
            piece = full.at[pl.ds(core * 16 + (px * Y + py) * nb, nb), part]
            to_core.append(remote(piece, piece, sib))

    def fold(acc, r, cols):
        return (acc[16 * r : 16 * (r + 1), cols] + acc[DT + 16 * r : DT + 16 * (r + 1), cols]).astype(BF)

    def edge_mid(b, carry):
        at = block(b)
        mask = row_mask(b, WIDTH)
        cot = gather(dst_col[at], 0, cots).astype(BF)
        picked_cot[at] = cot
        pre = inc[at] + nn(sm[at], wt2[...])
        sig = jax.nn.sigmoid(pre)
        out = jnp.where(mask, pre * sig, 0.0).astype(BF)
        slope[at] = jnp.where(mask, sig * (1.0 + pre * (1.0 - sig)), 0.0)
        acc_wb[...] += tn(out, cot)
        return carry

    lax.fori_loop(0, SLOTS // BLK, edge_mid, 0)
    for s in range(32):
        r, cols = s // 4, slice(128 * (s % 4), 128 * (s % 4 + 1))
        pieces_b[s] = acc_wb[64 * r : 64 * (r + 1), cols].astype(BF)
    b_core = remote(pieces_b.at[not_mine], rc_b, sib)

    def edge_grad(b, carry):
        at = block(b)
        grad = nt(picked_cot[at], wb[...]) * slope[at]
        slope[at] = grad
        grad = grad.astype(BF)
        dinc[at] = grad
        acc_wa[...] += tn(picked[at], grad)
        acc_wt[...] += tn(sm[at], grad)
        down[at] = nt(grad, wt2[...]).astype(BF)
        return carry

    lax.fori_loop(0, 2, edge_grad, 0)
    b_xy = reduce_core(b_core, pieces_b, rc_b, half_b, rx_b)
    lax.fori_loop(2, SLOTS // BLK, edge_grad, 0)

    for s in range(32):
        r, cols = s // 4, slice(128 * (s % 4), 128 * (s % 4 + 1))
        pieces_a[s, 0:64] = acc_wa[64 * r : 64 * (r + 1), cols].astype(BF)
        pieces_a[s, 64:80] = fold(acc_wt, r, cols) if s < 16 else jnp.zeros((16, 128), BF)
    a_core = remote(pieces_a.at[not_mine], rc_a, sib)

    def table_grad(owner, part, source):
        first = (4 + owner) * OWN if part == 0 else owner * OWN
        total = None
        for b in range(SLOTS // BLK):
            cols = slice(BLK * b, BLK * (b + 1))
            line = rows[0:1, cols]
            choice = jnp.concatenate(
                [pick_rows(line, first, OWN), pick_rows(line, first + 2 * OWN, OWN)], axis=0
            )
            term = nn(choice, source[cols])
            total = term if total is None else total + term
        return total.astype(BF).reshape(2, OWN, total.shape[1])

    def reduce_slot(part):
        ed[part] = (dt[part, 1 - zl].astype(F32) + rd[part, 1 - zl].astype(F32)).astype(BF)
        return remote(ed.at[part], re.at[part], zpart)

    def slot_sum(part):
        return dt[part, zl].astype(F32) + rd[part, zl].astype(F32) + re[part].astype(F32)

    dt_sib[0] = table_grad(1 - core, 0, dinc)
    rim_core = remote(dt_sib.at[0], rd.at[0], sib)
    a_xy = reduce_core(a_core, pieces_a, rc_a, half_a, rx_a)
    dt[0] = table_grad(core, 0, dinc)
    rim_core.wait_recv()
    rim_z = reduce_slot(0)

    pack(down)
    triplets(tout_col, tin_col, 2)
    unpack()

    def edge_back(b, carry):
        at = block(b)
        back = jnp.where(row_mask(b, 128), sm[at].astype(F32), 0.0).astype(BF)
        sm[at] = back
        acc_wd[...] += tn(back, inc[at].astype(BF))
        acc_wx[...] += tn(back, picked[at])
        return carry

    lax.fori_loop(0, SLOTS // BLK, edge_back, 0)
    for s in range(32):
        r, c = (s % 16) // 4, s % 4
        late[s] = fold(acc_wd if s < 16 else acc_wx, r, slice(128 * c, 128 * (c + 1)))
    l_core = remote(late.at[not_mine], rc_l, sib)

    b_z = send_z(sum_xy(b_xy, half_b, rx_b), rz_b)

    def edge_out(b, carry):
        at = block(b)
        dinc[at] = (slope[at] + nn(sm[at], wdown2[...])).astype(BF)
        return carry

    lax.fori_loop(0, SLOTS // BLK, edge_out, 0)
    l_xy = reduce_core(l_core, late, rc_l, half_l, rx_l)
    dt_sib[1] = table_grad(1 - core, 1, dinc)
    mid_core = remote(dt_sib.at[1], rd.at[1], sib)
    rim_z.wait_recv()
    rims_out[...] = slot_sum(0).astype(BF)
    to_tails = remote(rims_out.at[low], rims_in.at[0], below)
    to_heads = remote(rims_out.at[high], rims_in.at[1], above)
    a_z = send_z(sum_xy(a_xy, half_a, rx_a), rz_a)
    dt[1] = table_grad(core, 1, dinc)
    mid_core.wait_recv()
    mid_z = reduce_slot(1)
    nt_sib[...] = table_grad(1 - core, 0, sm)
    rim2_core = remote(nt_sib, nrd, sib)
    full_b[own_piece] = sum_z(b_z, rz_b)
    g_bxy, g_bcore = spread(full_b, pl.ds(0, 64))
    l_z = send_z(sum_xy(l_xy, half_l, rx_l), rz_l)
    ntd[...] = table_grad(core, 0, sm)
    rim2_core.wait_recv()
    ned[...] = (ntd[1 - zl].astype(F32) + nrd[1 - zl].astype(F32)).astype(BF)
    rim2_z = remote(ned, nre, zpart)

    main_rows, late_rows = pl.ds(0, 80), pl.ds(80, 16)
    full_a[own_piece, main_rows] = sum_z(a_z, rz_a)
    g_axy, g_acore = spread(full_a, main_rows)
    rim2_z.wait_recv()
    rims2_out[...] = (ntd[zl].astype(F32) + nrd[zl].astype(F32) + nre[...].astype(F32)).astype(BF)
    to_tails2 = remote(rims2_out.at[low], rims2_in.at[0], below)
    to_heads2 = remote(rims2_out.at[high], rims2_in.at[1], above)
    full_a[own_piece, late_rows] = sum_z(l_z, rz_l)
    g_lxy, g_lcore = spread(full_a, late_rows)
    forward(g_bxy, g_bcore, full_b, pl.ds(0, 64))
    for c in g_bcore:
        c.wait_recv()
    b_copy = pltpu.make_async_copy(full_b, full_b_out, local_sem.at[8])
    b_copy.start()
    forward(g_axy, g_acore, full_a, main_rows)
    forward(g_lxy, g_lcore, full_a, late_rows)

    mid_z.wait_recv()
    for c in (to_tails, to_heads, to_tails2, to_heads2):
        c.wait_recv()
    rims2 = jnp.concatenate([rims2_in[1], rims2_in[0]], axis=0)
    dproj = slot_sum(1) + jnp.concatenate([rims_in[1].astype(F32), rims_in[0].astype(F32)], axis=0)
    dproj = dproj + nn(rims2, wdown2[...])
    coarse = dproj.astype(BF)
    fine = (dproj - coarse.astype(F32)).astype(BF)
    grad[...] = (nt(coarse, wa[...]) + nt(fine, wa[...])).astype(BF)
    grad_copy = pltpu.make_async_copy(grad, grad_out, local_sem.at[6])
    grad_copy.start()

    for c in g_acore + g_lcore:
        c.wait_recv()
    a_copy = pltpu.make_async_copy(full_a, full_a_out, local_sem.at[7])
    a_copy.start()
    for c in started:
        c.wait_send()
    b_copy.wait()
    grad_copy.wait()
    a_copy.wait()


def finish(
    factor, grad_hbm, full_a_hbm, full_b_hbm, wdown_ref, gatoms_hbm, gwa_hbm, gwd_hbm, gwt_hbm, gwb_hbm,
    full_a, full_b, grad, gwa, gwd, gwt, gwb, sem,
):
    copies = []

    def copy(src, dst):
        c = pltpu.make_async_copy(src, dst, sem.at[len(copies)])
        c.start()
        copies.append(c)
        return c

    loads_b = [copy(full_b_hbm.at[pl.ds(16 * i, 16)], full_b.at[pl.ds(16 * i, 16)]) for i in range(2)]
    loads_a = [copy(full_a_hbm.at[pl.ds(16 * i, 16)], full_a.at[pl.ds(16 * i, 16)]) for i in range(2)]
    through = copy(grad_hbm, grad)
    loaded = len(copies)

    def rows_of(full, s, part):
        return jnp.concatenate([full[s + c, part].astype(F32) for c in range(4)], axis=1)

    for i in range(2):
        loads_b[i].wait()
        for r in range(4 * i, 4 * i + 4):
            gwb[64 * r : 64 * (r + 1)] = rows_of(full_b, 4 * r, slice(0, 64)) * factor
        copy(gwb.at[pl.ds(256 * i, 256)], gwb_hbm.at[pl.ds(256 * i, 256)])
    for c in loads_a:
        c.wait()
    back = jnp.concatenate([rows_of(full_a, 16 + 4 * r, slice(80, 96)) for r in range(4)], axis=0)
    back = tn(back.astype(BF), wdown_ref[...])
    for i in range(2):
        for r in range(4 * i, 4 * i + 4):
            main = rows_of(full_a, 4 * r, slice(0, 64))
            gwa[64 * r : 64 * (r + 1)] = (main + back[64 * r : 64 * (r + 1)]) * factor
        copy(gwa.at[pl.ds(256 * i, 256)], gwa_hbm.at[pl.ds(256 * i, 256)])
    for r in range(4):
        gwt[16 * r : 16 * (r + 1)] = rows_of(full_a, 4 * r, slice(64, 80)) * factor
        gwd[16 * r : 16 * (r + 1)] = rows_of(full_a, 4 * r, slice(80, 96)) * factor
    copy(gwt, gwt_hbm)
    copy(gwd, gwd_hbm)
    through.wait()
    copy(grad, gatoms_hbm)
    for c in copies[loaded:]:
        c.wait()


def per_device(
    slabs, groups,
    atoms, messages, edge_src, edge_dst, trip_in, trip_out, trip_basis, edge_count, trip_count,
    w_a, w_down, w_t, w_b, cotangent,
):
    dims = dims_of(slabs)
    Y, ZH, X = dims
    XY, Z = X * Y, 2 * ZH
    nb = 16 // XY
    transfers = 48 + 9 * (XY - 1) + 3 * (Z - 1)
    vmem = pl.BlockSpec(memory_space=pltpu.VMEM)
    hbm = pl.BlockSpec(memory_space=pl.ANY)
    index = [a.reshape(16, 128) for a in (edge_src, edge_dst, trip_in, trip_out)]
    w_down = w_down.T
    V = pltpu.VMEM
    full_a, full_b, grad = pl.pallas_call(
        functools.partial(kernel, dims),
        out_shape=(
            jax.ShapeDtypeStruct((32, 96, 128), BF),
            jax.ShapeDtypeStruct((32, 64, 128), BF),
            jax.ShapeDtypeStruct((OWN, WIDTH), BF),
        ),
        in_specs=[vmem] * 8 + [hbm] * 6,
        out_specs=(hbm, hbm, hbm),
        scratch_shapes=[
            V((4, OWN, WIDTH), BF), V((4, OWN, WIDTH), BF), V((4, OWN, WIDTH), BF),
            V((SLOTS, WIDTH), BF), V((DT, SLOTS), BF), V((512, WIDTH), BF), V((512, WIDTH), BF),
            V((SLOTS, WIDTH), BF), V((SLOTS, WIDTH), F32), V((SLOTS, WIDTH), BF),
            V((SLOTS, 128), jnp.int32), V((SLOTS, 128), jnp.int32),
            V((SLOTS, 128), jnp.int32), V((SLOTS, 128), jnp.int32),
            V((8, SLOTS), jnp.int32), V((SLOTS, 128), F32), V((128, WIDTH), BF), V((128, WIDTH), BF),
            V((SLOTS, 128), BF), V((LO, WIDTH), BF), V((LO, WIDTH), F32), V((SLOTS, 128), BF),
            V((2, 2, OWN, WIDTH), BF), V((2, 2, OWN, WIDTH), BF), V((2, 2, OWN, WIDTH), BF),
            V((2, OWN, WIDTH), BF), V((2, OWN, WIDTH), BF), V((OWN, WIDTH), BF),
            V((OWN, WIDTH), BF), V((2, GH, WIDTH), BF),
            V((2, OWN, 128), BF), V((2, OWN, 128), BF), V((2, OWN, 128), BF),
            V((OWN, 128), BF), V((OWN, 128), BF), V((OWN, 128), BF), V((2, GH, 128), BF),
            V((512, WIDTH), F32), V((512, WIDTH), F32), V((128, WIDTH), F32), V((128, WIDTH), F32),
            V((128, WIDTH), F32),
            V((SLOTS, WIDTH), BF), V((SLOTS, WIDTH), F32),
            V((32, 64, 128), BF), V((16, 64, 128), BF), V((16, 64, 128), BF), V((XY - 1, nb, 64, 128), BF),
            V((Z, nb, 64, 128), BF), V((32, 64, 128), BF),
            V((32, 80, 128), BF), V((16, 80, 128), BF), V((16, 80, 128), BF), V((XY - 1, nb, 80, 128), BF),
            V((Z, nb, 80, 128), BF), V((32, 96, 128), BF),
            V((32, 16, 128), BF), V((16, 16, 128), BF), V((16, 16, 128), BF), V((XY - 1, nb, 16, 128), BF),
            V((Z, nb, 16, 128), BF),
            pltpu.SemaphoreType.DMA((transfers,)), pltpu.SemaphoreType.DMA((transfers,)),
            pltpu.SemaphoreType.DMA((9,)),
        ],
        compiler_params=pltpu.CompilerParams(
            collective_id=0, has_side_effects=True, vmem_limit_bytes=60 * 1024 * 1024
        ),
    )(
        edge_count.reshape(1, 1), trip_count.reshape(1, 1), *index, w_down, w_t,
        atoms, cotangent, messages, trip_basis.T, w_a, w_b,
    )
    factor = 1.0 / math.sqrt(OWN * groups * slabs)
    grad, gwa, gwd, gwt, gwb = pl.pallas_call(
        functools.partial(finish, factor),
        out_shape=(
            jax.ShapeDtypeStruct((OWN, WIDTH), BF),
            jax.ShapeDtypeStruct((512, WIDTH), F32),
            jax.ShapeDtypeStruct((DT, WIDTH), F32),
            jax.ShapeDtypeStruct((DT, WIDTH), F32),
            jax.ShapeDtypeStruct((512, WIDTH), F32),
        ),
        in_specs=[hbm, hbm, hbm, vmem],
        out_specs=(hbm,) * 5,
        scratch_shapes=[
            V((32, 96, 128), BF), V((32, 64, 128), BF), V((OWN, WIDTH), BF), V((512, WIDTH), F32),
            V((DT, WIDTH), F32), V((DT, WIDTH), F32), V((512, WIDTH), F32), pltpu.SemaphoreType.DMA((12,)),
        ],
        compiler_params=pltpu.CompilerParams(vmem_limit_bytes=60 * 1024 * 1024),
    )(grad, full_a, full_b, w_down)
    return grad, gwa, gwd.T, gwt, gwb


def solution(mesh):
    both = P(("dom", "gp"))
    rows = P(("dom", "gp"), None)
    in_specs = (rows, rows, both, both, both, both, rows, both, both, P(), P(), P(), P(), rows)
    out_specs = (rows, P(), P(), P(), P())
    return jax.shard_map(
        functools.partial(per_device, mesh.shape["dom"], mesh.shape["gp"]),
        mesh=mesh, in_specs=in_specs, out_specs=out_specs, check_vma=False,
    )
```

```python
import functools
import math

import jax
import jax.numpy as jnp
from jax import lax
from jax.experimental import pallas as pl
from jax.experimental.pallas import tpu as pltpu
from jax.sharding import PartitionSpec as P

BF = jnp.bfloat16
F32 = jnp.float32
MESH = pl.DeviceIdType.MESH
GH = 128
OWN = 256
SLOTS = 2048
WIDTH = 512
DT = 64
LO = 256
BLK = 512


def dims_of(slabs):
    return {64: (4, 4, 4), 4: (1, 1, 4), 2: (1, 1, 2)}[slabs]


def nn(a, b):
    return lax.dot_general(a, b, (((1,), (0,)), ((), ())), preferred_element_type=F32)


def nt(a, b):
    return lax.dot_general(a, b, (((1,), (1,)), ((), ())), preferred_element_type=F32)


def tn(a, b):
    return lax.dot_general(a, b, (((0,), (0,)), ((), ())), preferred_element_type=F32)


def lanes(shape):
    return lax.broadcasted_iota(jnp.int32, shape, len(shape) - 1)


def pick_columns(index, first, width):
    lane = lanes(index.shape)
    local = index - first
    return jnp.concatenate(
        [jnp.where(local == lane + 128 * j, 1.0, 0.0).astype(BF) for j in range(width // 128)], axis=1
    )


def pick_rows(index, first, height):
    shape = (height, index.shape[1])
    row = lax.broadcasted_iota(jnp.int32, shape, 0)
    return jnp.where(row == jnp.broadcast_to(index - first, shape), 1.0, 0.0).astype(BF)


def table_row(src):
    up = src - 1536
    lower = 4 * OWN + ((src >> 7) << 8) + (src & 127)
    upper = 4 * OWN + ((up >> 7) << 8) + GH + (up & 127)
    return jnp.where(src < 512, lower, jnp.where(src < 1536, src - 512, upper))


def kernel(
    dims,
    ecnt_ref, tcnt_ref, src_ref, dst_ref, tin_ref, tout_ref, wdown_ref, wt_ref,
    atoms_hbm, cot_hbm, msg_hbm, basis_hbm, wa_hbm, wb_hbm,
    full_a_out, full_b_out, grad_out,
    mid, rim, cots, msg, basis, wa, wb, picked, inc, dinc,
    src_col, dst_col, tin_col, tout_col, rows, basis2, wdown2, wt2,
    down, dn, acc_s, sm,
    dt_sib, dt, rd, ed, re, grad, rims_out, rims_in,
    acc_wa, acc_wb, acc_wt, acc_wd, acc_wx, picked_cot, slope,
    pieces_b, rc_b, half_b, rx_b, rz_b, full_b,
    pieces_a, rc_a, half_a, rx_a, rz_a, full_a,
    late, rc_l, half_l, rx_l, rz_l,
    send, recv, local_sem,
):
    Y, ZH, X = dims
    XY = X * Y
    Z = 2 * ZH
    nb = 16 // XY
    dom = lax.axis_index("dom")
    gp = lax.axis_index("gp")
    slabs = Y * ZH * X
    x = lax.rem(dom, X)
    zh = lax.rem(lax.div(dom, X), ZH)
    y = lax.div(dom, X * ZH)
    core = lax.rem(gp, 2)
    zl = lax.div(gp, 2)
    z = zh * 2 + zl

    sib = {"dom": dom, "gp": zl * 2 + (1 - core)}
    zpart = {"dom": dom, "gp": (1 - zl) * 2 + core}
    kz = (1 - zl) * 2 + core
    above = {"dom": lax.rem(dom + 1, slabs), "gp": gp}
    below = {"dom": lax.rem(dom + slabs - 1, slabs), "gp": gp}
    xy_peers = []
    for j in range(1, XY):
        px = lax.rem(x + j // Y, X)
        py = lax.rem(y + j % Y, Y)
        xy_peers.append((px * Y + py, {"dom": (py * ZH + zh) * X + px, "gp": gp}))
    z_peers = []
    for j in range(1, Z):
        pz = lax.rem(z + j, Z)
        z_peers.append({"dom": (y * ZH + lax.div(pz, 2)) * X + x, "gp": lax.rem(pz, 2) * 2 + core})

    barrier = pltpu.get_barrier_semaphore()
    others = [sib, above, below] + [d for _, d in xy_peers] + z_peers
    for d in others:
        pl.semaphore_signal(barrier, inc=1, device_id=d, device_id_type=MESH)

    count = [0]
    started = []

    def remote(src, dst, device):
        i = count[0]
        count[0] += 1
        c = pltpu.make_async_remote_copy(
            src_ref=src, dst_ref=dst, send_sem=send.at[i], recv_sem=recv.at[i],
            device_id=device, device_id_type=MESH,
        )
        c.start()
        started.append(c)
        return c

    local = []
    for i, (src, dst) in enumerate(
        (
            (atoms_hbm, mid.at[gp]), (cot_hbm, cots.at[gp]), (basis_hbm, basis),
            (wa_hbm, wa), (msg_hbm, msg), (wb_hbm, wb),
        )
    ):
        c = pltpu.make_async_copy(src, dst, local_sem.at[i])
        c.start()
        local.append(c)
    atoms_in, cot_in, basis_in, wa_in, msg_in, wb_in = local

    pl.semaphore_wait(barrier, len(others))

    low = pl.ds(0, GH)
    high = pl.ds(GH, GH)
    to_above = remote(atoms_hbm.at[high], rim.at[gp, low], above)
    to_below = remote(atoms_hbm.at[low], rim.at[gp, high], below)
    to_z = remote(atoms_hbm, mid.at[gp], zpart)
    to_sib = remote(atoms_hbm, mid.at[gp], sib)

    edges = ecnt_ref[...]
    trips = tcnt_ref[...]
    for n, (ref, col) in enumerate(
        ((src_ref, src_col), (dst_ref, dst_col), (tin_ref, tin_col), (tout_ref, tout_col))
    ):
        flat = ref[...]
        if n == 0:
            flat = table_row(flat)
        for j in range(SLOTS // 128):
            line = flat[j : j + 1]
            rows[n : n + 1, 128 * j : 128 * (j + 1)] = line
            col[128 * j : 128 * (j + 1)] = jnp.transpose(jnp.broadcast_to(line, (128, 128)))
    wdown2[...] = jnp.concatenate([wdown_ref[...], wdown_ref[...]], axis=0)
    wt2[...] = jnp.concatenate([wt_ref[...], wt_ref[...]], axis=0)
    basis_in.wait()
    twice = jnp.where(
        lax.broadcasted_iota(jnp.int32, (DT, 128), 0) == (lanes((DT, 128)) & (DT - 1)), 1.0, 0.0
    ).astype(BF)
    valid = lax.broadcasted_iota(jnp.int32, (SLOTS, 128), 0) < jnp.broadcast_to(trips, (SLOTS, 128))
    basis2[...] = jnp.where(valid, tn(basis[...], twice), 0.0)

    atoms_in.wait()
    to_sib.wait_recv()
    to_above.wait_recv()
    z_low = remote(rim.at[gp, low], rim.at[gp, low], zpart)
    s_low = remote(rim.at[gp, low], rim.at[gp, low], sib)
    to_below.wait_recv()
    z_high = remote(rim.at[gp, high], rim.at[gp, high], zpart)
    s_high = remote(rim.at[gp, high], rim.at[gp, high], sib)
    z_cot = remote(cot_hbm, cots.at[gp], zpart)
    s_cot = remote(cot_hbm, cots.at[gp], sib)
    to_z.wait_recv()
    f_mid = remote(mid.at[kz], mid.at[kz], sib)
    f_mid.wait_recv()

    def block(b):
        return pl.ds(pl.multiple_of(b * BLK, BLK), BLK)

    def gather(index, first, source):
        return nn(pick_columns(index, first, 4 * OWN), source[...].reshape(4 * OWN, WIDTH))

    def edge_own(b, carry):
        picked[block(b)] = gather(src_col[block(b)], 0, mid).astype(BF)
        return carry

    lax.fori_loop(0, SLOTS // BLK, edge_own, 0)

    z_low.wait_recv()
    f_low = remote(rim.at[kz, low], rim.at[kz, low], sib)
    z_high.wait_recv()
    f_high = remote(rim.at[kz, high], rim.at[kz, high], sib)
    for c in (s_low, s_high, f_low, f_high):
        c.wait_recv()
    wa_in.wait()
    msg_in.wait()

    def row_mask(b, width):
        shape = (BLK, width)
        return lax.broadcasted_iota(jnp.int32, shape, 0) < jnp.broadcast_to(edges - b * BLK, shape)

    def edge_in(b, carry):
        at = block(b)
        got = (picked[at].astype(F32) + gather(src_col[at], 4 * OWN, rim)).astype(BF)
        picked[at] = got
        proj = nn(got, wa[...]).astype(BF).astype(F32)
        value = jnp.where(row_mask(b, WIDTH), proj + msg[at].astype(F32), 0.0)
        inc[at] = value
        down[at] = nt(value.astype(BF), wdown2[...]).astype(BF)
        return carry

    lax.fori_loop(0, SLOTS // BLK, edge_in, 0)
    z_cot.wait_recv()
    f_cot = remote(cots.at[kz], cots.at[kz], sib)

    def pack(source):
        first = lanes((LO, 128)) < DT
        for j in range(4):
            a = source[2 * j * LO : (2 * j + 1) * LO].astype(F32)
            b = source[(2 * j + 1) * LO : (2 * j + 2) * LO].astype(F32)
            dn[:, 128 * j : 128 * (j + 1)] = jnp.where(first, a, b).astype(BF)

    def unpack():
        first = lanes((LO, 128)) < DT
        for j in range(4):
            v = acc_s[:, 128 * j : 128 * (j + 1)]
            sm[2 * j * LO : (2 * j + 1) * LO] = jnp.where(first, v, 0.0).astype(BF)
            sm[(2 * j + 1) * LO : (2 * j + 2) * LO] = jnp.where(first, 0.0, v).astype(BF)

    def triplets(from_col, to_col, to_row, between=lambda: None):
        half_lane = jnp.where(lanes((BLK, 128)) < DT, 0, 1)
        acc_s[...] = jnp.zeros_like(acc_s)

        def body(b, carry):
            at = block(b)
            frm = from_col[at]
            to = to_col[at]
            got = nn(pick_columns(frm & (LO - 1), 0, LO), dn[...])
            frm_hi = frm >> 8
            to_hi = to >> 8
            value = jnp.where(frm_hi == half_lane, got[:, 0:128], 0.0)
            for j in range(1, 4):
                value = value + jnp.where(
                    frm_hi == half_lane + 2 * j, got[:, 128 * j : 128 * (j + 1)], 0.0
                )
            value = value + pltpu.roll(value, DT, 1)
            value = value * basis2[at]
            spread = jnp.concatenate(
                [jnp.where(to_hi == half_lane + 2 * j, value, 0.0).astype(BF) for j in range(4)], axis=1
            )
            line = rows[to_row : to_row + 1, block(b)]
            acc_s[...] += nn(pick_rows(line & (LO - 1), 0, LO), spread)
            return carry

        lax.fori_loop(0, 2, body, 0)
        result = between()
        lax.fori_loop(2, SLOTS // BLK, body, 0)
        return result

    pack(down)
    triplets(tin_col, tout_col, 3)
    unpack()
    cot_in.wait()
    wb_in.wait()
    s_cot.wait_recv()
    f_cot.wait_recv()

    for acc in (acc_wa, acc_wb, acc_wt, acc_wd, acc_wx):
        acc[...] = jnp.zeros_like(acc)

    not_mine = pl.ds((1 - core) * 16, 16)
    mine = pl.ds(core * 16, 16)
    own_s = x * Y + y
    own_nb = pl.ds(own_s * nb, nb)
    own_piece = pl.ds(core * 16 + own_s * nb, nb)

    def reduce_core(copy, pieces, received, half, got):
        copy.wait_recv()
        half[...] = (pieces[mine].astype(F32) + received[...].astype(F32)).astype(BF)
        return [
            remote(half.at[pl.ds(s * nb, nb)], got.at[j], d) for j, (s, d) in enumerate(xy_peers)
        ]

    def sum_xy(copies, half, got):
        for c in copies:
            c.wait_recv()
        total = half[own_nb].astype(F32)
        for j in range(XY - 1):
            total = total + got[j].astype(F32)
        return total

    def send_z(own, got):
        got[0] = own.astype(BF)
        return [remote(got.at[0], got.at[j + 1], d) for j, d in enumerate(z_peers)]

    def sum_z(copies, got):
        for c in copies:
            c.wait_recv()
        total = got[lax.rem(Z - z, Z)].astype(F32)
        for j in range(1, Z):
            total = total + got[lax.rem(j + Z - z, Z)].astype(F32)
        return total.astype(BF)

    def spread(full):
        own = full.at[own_piece]
        return [remote(own, own, d) for _, d in xy_peers], [remote(own, own, sib)]

    def forward(copies, to_core, full):
        for j, c in enumerate(copies):
            c.wait_recv()
            px = lax.rem(x + X - (j + 1) // Y, X)
            py = lax.rem(y + Y - (j + 1) % Y, Y)
            piece = full.at[pl.ds(core * 16 + (px * Y + py) * nb, nb)]
            to_core.append(remote(piece, piece, sib))

    def fold(acc, r, cols):
        return (acc[16 * r : 16 * (r + 1), cols] + acc[DT + 16 * r : DT + 16 * (r + 1), cols]).astype(BF)

    def edge_mid(b, carry):
        at = block(b)
        mask = row_mask(b, WIDTH)
        cot = gather(dst_col[at], 0, cots).astype(BF)
        picked_cot[at] = cot
        pre = inc[at] + nn(sm[at], wt2[...])
        sig = jax.nn.sigmoid(pre)
        out = jnp.where(mask, pre * sig, 0.0).astype(BF)
        slope[at] = jnp.where(mask, sig * (1.0 + pre * (1.0 - sig)), 0.0)
        acc_wb[...] += tn(out, cot)
        return carry

    lax.fori_loop(0, SLOTS // BLK, edge_mid, 0)
    for s in range(32):
        r, cols = s // 4, slice(128 * (s % 4), 128 * (s % 4 + 1))
        pieces_b[s] = acc_wb[64 * r : 64 * (r + 1), cols].astype(BF)
    b_core = remote(pieces_b.at[not_mine], rc_b, sib)

    def edge_grad(b, carry):
        at = block(b)
        grad = nt(picked_cot[at], wb[...]) * slope[at]
        slope[at] = grad
        grad = grad.astype(BF)
        acc_wa[...] += tn(picked[at], grad)
        acc_wt[...] += tn(sm[at], grad)
        down[at] = nt(grad, wt2[...]).astype(BF)
        return carry

    lax.fori_loop(0, 2, edge_grad, 0)
    b_xy = reduce_core(b_core, pieces_b, rc_b, half_b, rx_b)
    lax.fori_loop(2, SLOTS // BLK, edge_grad, 0)

    for s in range(32):
        r, cols = s // 4, slice(128 * (s % 4), 128 * (s % 4 + 1))
        pieces_a[s, 0:64] = acc_wa[64 * r : 64 * (r + 1), cols].astype(BF)
        pieces_a[s, 64:80] = fold(acc_wt, r, cols) if s < 16 else jnp.zeros((16, 128), BF)
    a_core = remote(pieces_a.at[not_mine], rc_a, sib)

    pack(down)
    a_xy = triplets(
        tout_col, tin_col, 2, lambda: reduce_core(a_core, pieces_a, rc_a, half_a, rx_a)
    )
    unpack()

    def edge_out(b, carry):
        at = block(b)
        mask = row_mask(b, 128)
        back = jnp.where(mask, sm[at].astype(F32), 0.0).astype(BF)
        dinc[at] = (slope[at] + nn(back, wdown2[...])).astype(BF)
        acc_wd[...] += tn(back, inc[at].astype(BF))
        acc_wx[...] += tn(back, picked[at])
        return carry

    lax.fori_loop(0, SLOTS // BLK, edge_out, 0)
    for s in range(32):
        r, c = (s % 16) // 4, s % 4
        late[s] = fold(acc_wd if s < 16 else acc_wx, r, slice(128 * c, 128 * (c + 1)))
    l_core = remote(late.at[not_mine], rc_l, sib)

    def table_grad(owner, part, out):
        first = (4 + owner) * OWN if part == 0 else owner * OWN
        line = rows[0:1, :]
        choice = jnp.concatenate(
            [pick_rows(line, first, OWN), pick_rows(line, first + 2 * OWN, OWN)], axis=0
        )
        total = nn(choice, dinc[...]).astype(BF)
        out[part, 0] = total[0:OWN]
        out[part, 1] = total[OWN:]

    def reduce_slot(part):
        ed[part] = (dt[part, 1 - zl].astype(F32) + rd[part, 1 - zl].astype(F32)).astype(BF)
        return remote(ed.at[part], re.at[part], zpart)

    def slot_sum(part):
        return dt[part, zl].astype(F32) + rd[part, zl].astype(F32) + re[part].astype(F32)

    table_grad(1 - core, 0, dt_sib)
    rim_core = remote(dt_sib.at[0], rd.at[0], sib)
    rz = send_z(sum_xy(b_xy, half_b, rx_b), rz_b)
    table_grad(core, 0, dt)
    l_xy = reduce_core(l_core, late, rc_l, half_l, rx_l)
    rim_core.wait_recv()
    rim_z = reduce_slot(0)
    table_grad(1 - core, 1, dt_sib)
    mid_core = remote(dt_sib.at[1], rd.at[1], sib)
    a_z = send_z(sum_xy(a_xy, half_a, rx_a), rz_a)
    table_grad(core, 1, dt)
    full_b[own_piece] = sum_z(rz, rz_b)
    g_bxy, g_bcore = spread(full_b)
    l_z = send_z(sum_xy(l_xy, half_l, rx_l), rz_l)
    mid_core.wait_recv()
    mid_z = reduce_slot(1)

    rim_z.wait_recv()
    rims_out[...] = slot_sum(0).astype(BF)
    to_tails = remote(rims_out.at[low], rims_in.at[0], below)
    to_heads = remote(rims_out.at[high], rims_in.at[1], above)

    full_a[own_piece, 0:80] = sum_z(a_z, rz_a)
    full_a[own_piece, 80:96] = sum_z(l_z, rz_l)
    g_axy, g_acore = spread(full_a)
    forward(g_bxy, g_bcore, full_b)
    for c in g_bcore:
        c.wait_recv()
    b_copy = pltpu.make_async_copy(full_b, full_b_out, local_sem.at[8])
    b_copy.start()
    forward(g_axy, g_acore, full_a)
    own_copy = pltpu.make_async_copy(full_a.at[mine], full_a_out.at[mine], local_sem.at[9])
    own_copy.start()

    mid_z.wait_recv()
    to_tails.wait_recv()
    to_heads.wait_recv()
    dproj = slot_sum(1) + jnp.concatenate([rims_in[1].astype(F32), rims_in[0].astype(F32)], axis=0)
    coarse = dproj.astype(BF)
    fine = (dproj - coarse.astype(F32)).astype(BF)
    grad[...] = (nt(coarse, wa[...]) + nt(fine, wa[...])).astype(BF)
    grad_copy = pltpu.make_async_copy(grad, grad_out, local_sem.at[6])
    grad_copy.start()

    for c in g_acore:
        c.wait_recv()
    a_copy = pltpu.make_async_copy(full_a.at[not_mine], full_a_out.at[not_mine], local_sem.at[7])
    a_copy.start()
    for c in started:
        c.wait_send()
    b_copy.wait()
    grad_copy.wait()
    a_copy.wait()
    own_copy.wait()


def finish(
    factor, grad_hbm, full_a_hbm, full_b_hbm, wdown_ref, gatoms_hbm, gwa_hbm, gwd_hbm, gwt_hbm, gwb_hbm,
    full_a, full_b, grad, gwa, gwd, gwt, gwb, sem,
):
    copies = []

    def copy(src, dst):
        c = pltpu.make_async_copy(src, dst, sem.at[len(copies)])
        c.start()
        copies.append(c)
        return c

    loads_b = [copy(full_b_hbm.at[pl.ds(16 * i, 16)], full_b.at[pl.ds(16 * i, 16)]) for i in range(2)]
    loads_a = [copy(full_a_hbm.at[pl.ds(16 * i, 16)], full_a.at[pl.ds(16 * i, 16)]) for i in range(2)]
    through = copy(grad_hbm, grad)
    loaded = len(copies)

    def rows_of(full, s, part):
        return jnp.concatenate([full[s + c, part].astype(F32) for c in range(4)], axis=1)

    for i in range(2):
        loads_b[i].wait()
        for r in range(4 * i, 4 * i + 4):
            gwb[64 * r : 64 * (r + 1)] = rows_of(full_b, 4 * r, slice(0, 64)) * factor
        copy(gwb.at[pl.ds(256 * i, 256)], gwb_hbm.at[pl.ds(256 * i, 256)])
    for c in loads_a:
        c.wait()
    back = jnp.concatenate([rows_of(full_a, 16 + 4 * r, slice(80, 96)) for r in range(4)], axis=0)
    back = tn(back.astype(BF), wdown_ref[...])
    for i in range(2):
        for r in range(4 * i, 4 * i + 4):
            main = rows_of(full_a, 4 * r, slice(0, 64))
            gwa[64 * r : 64 * (r + 1)] = (main + back[64 * r : 64 * (r + 1)]) * factor
        copy(gwa.at[pl.ds(256 * i, 256)], gwa_hbm.at[pl.ds(256 * i, 256)])
    for r in range(4):
        gwt[16 * r : 16 * (r + 1)] = rows_of(full_a, 4 * r, slice(64, 80)) * factor
        gwd[16 * r : 16 * (r + 1)] = rows_of(full_a, 4 * r, slice(80, 96)) * factor
    copy(gwt, gwt_hbm)
    copy(gwd, gwd_hbm)
    through.wait()
    copy(grad, gatoms_hbm)
    for c in copies[loaded:]:
        c.wait()


def per_device(
    slabs, groups,
    atoms, messages, edge_src, edge_dst, trip_in, trip_out, trip_basis, edge_count, trip_count,
    w_a, w_down, w_t, w_b, cotangent,
):
    dims = dims_of(slabs)
    Y, ZH, X = dims
    XY, Z = X * Y, 2 * ZH
    nb = 16 // XY
    transfers = 40 + 7 * (XY - 1) + 5 * (Z - 1)
    vmem = pl.BlockSpec(memory_space=pltpu.VMEM)
    hbm = pl.BlockSpec(memory_space=pl.ANY)
    index = [a.reshape(16, 128) for a in (edge_src, edge_dst, trip_in, trip_out)]
    w_down = w_down.T
    V = pltpu.VMEM
    full_a, full_b, grad = pl.pallas_call(
        functools.partial(kernel, dims),
        out_shape=(
            jax.ShapeDtypeStruct((32, 96, 128), BF),
            jax.ShapeDtypeStruct((32, 64, 128), BF),
            jax.ShapeDtypeStruct((OWN, WIDTH), BF),
        ),
        in_specs=[vmem] * 8 + [hbm] * 6,
        out_specs=(hbm, hbm, hbm),
        scratch_shapes=[
            V((4, OWN, WIDTH), BF), V((4, OWN, WIDTH), BF), V((4, OWN, WIDTH), BF),
            V((SLOTS, WIDTH), BF), V((DT, SLOTS), BF), V((512, WIDTH), BF), V((512, WIDTH), BF),
            V((SLOTS, WIDTH), BF), V((SLOTS, WIDTH), F32), V((SLOTS, WIDTH), BF),
            V((SLOTS, 128), jnp.int32), V((SLOTS, 128), jnp.int32),
            V((SLOTS, 128), jnp.int32), V((SLOTS, 128), jnp.int32),
            V((8, SLOTS), jnp.int32), V((SLOTS, 128), F32), V((128, WIDTH), BF), V((128, WIDTH), BF),
            V((SLOTS, 128), BF), V((LO, WIDTH), BF), V((LO, WIDTH), F32), V((SLOTS, 128), BF),
            V((2, 2, OWN, WIDTH), BF), V((2, 2, OWN, WIDTH), BF), V((2, 2, OWN, WIDTH), BF),
            V((2, OWN, WIDTH), BF), V((2, OWN, WIDTH), BF), V((OWN, WIDTH), BF),
            V((OWN, WIDTH), BF), V((2, GH, WIDTH), BF),
            V((512, WIDTH), F32), V((512, WIDTH), F32), V((128, WIDTH), F32), V((128, WIDTH), F32),
            V((128, WIDTH), F32),
            V((SLOTS, WIDTH), BF), V((SLOTS, WIDTH), F32),
            V((32, 64, 128), BF), V((16, 64, 128), BF), V((16, 64, 128), BF), V((XY - 1, nb, 64, 128), BF),
            V((Z, nb, 64, 128), BF), V((32, 64, 128), BF),
            V((32, 80, 128), BF), V((16, 80, 128), BF), V((16, 80, 128), BF), V((XY - 1, nb, 80, 128), BF),
            V((Z, nb, 80, 128), BF), V((32, 96, 128), BF),
            V((32, 16, 128), BF), V((16, 16, 128), BF), V((16, 16, 128), BF), V((XY - 1, nb, 16, 128), BF),
            V((Z, nb, 16, 128), BF),
            pltpu.SemaphoreType.DMA((transfers,)), pltpu.SemaphoreType.DMA((transfers,)),
            pltpu.SemaphoreType.DMA((10,)),
        ],
        compiler_params=pltpu.CompilerParams(
            collective_id=0, has_side_effects=True, vmem_limit_bytes=60 * 1024 * 1024
        ),
    )(
        edge_count.reshape(1, 1), trip_count.reshape(1, 1), *index, w_down, w_t,
        atoms, cotangent, messages, trip_basis.T, w_a, w_b,
    )
    factor = 1.0 / math.sqrt(OWN * groups * slabs)
    grad, gwa, gwd, gwt, gwb = pl.pallas_call(
        functools.partial(finish, factor),
        out_shape=(
            jax.ShapeDtypeStruct((OWN, WIDTH), BF),
            jax.ShapeDtypeStruct((512, WIDTH), F32),
            jax.ShapeDtypeStruct((DT, WIDTH), F32),
            jax.ShapeDtypeStruct((DT, WIDTH), F32),
            jax.ShapeDtypeStruct((512, WIDTH), F32),
        ),
        in_specs=[hbm, hbm, hbm, vmem],
        out_specs=(hbm,) * 5,
        scratch_shapes=[
            V((32, 96, 128), BF), V((32, 64, 128), BF), V((OWN, WIDTH), BF), V((512, WIDTH), F32),
            V((DT, WIDTH), F32), V((DT, WIDTH), F32), V((512, WIDTH), F32), pltpu.SemaphoreType.DMA((12,)),
        ],
        compiler_params=pltpu.CompilerParams(vmem_limit_bytes=60 * 1024 * 1024),
    )(grad, full_a, full_b, w_down)
    return grad, gwa, gwd.T, gwt, gwb


def solution(mesh):
    both = P(("dom", "gp"))
    rows = P(("dom", "gp"), None)
    in_specs = (rows, rows, both, both, both, both, rows, both, both, P(), P(), P(), P(), rows)
    out_specs = (rows, P(), P(), P(), P())
    return jax.shard_map(
        functools.partial(per_device, mesh.shape["dom"], mesh.shape["gp"]),
        mesh=mesh, in_specs=in_specs, out_specs=out_specs, check_vma=False,
    )
```
